128 devices in a mesh: lon: 16 (over z_hi, x, core), lat: 8 (over z_lo, y).
Axes of the slice: x: 4, y: 4, z: 4 (z_hi: 2, z_lo: 2; z = z_hi * 2 + z_lo), core: 2. Of those that a mesh axis runs over, the one named last changes fastest.
Arguments:
- fields: bfloat16 [2, 192, 384, 512], P(None, 'lat', 'lon'), may hold values from -6 to 6
- cotangent: bfloat16 [2, 192, 384, 512], P(None, 'lat', 'lon'), may hold values from -6 to 6
- qkv_weight: bfloat16 [512, 1536], replicated, may hold values from -1 to 1, as said below
- out_weight: bfloat16 [512, 512], replicated, may hold values from -0.25 to 0.25
Outputs:
- output_field: bfloat16 [2, 192, 384, 512], P(None, 'lat', 'lon')
- field_grad: bfloat16 [2, 192, 384, 512], P(None, 'lat', 'lon')
- qkv_grad: float32 [512, 1536], P(('lon', 'lat'))
- out_grad: float32 [512, 512], P(('lon', 'lat'))
The draws below stay inside these ranges and needn't reach their ends.
Inputs may be any that keep to these rules, and one draw needn't show every extreme that they name: `qkv_weight`: a dense projection matrix, about 512^-0.5 in scale.
All inputs are finite; a program needn't handle non-finite values.
Results may differ from the reference program's by a relative error of at most 0.015.
Values may be sent and summed in bfloat16 or wider, within the bound.
A program may use at most 192 MiB of HBM per device.

```python
import jax
import jax.numpy as jnp
from jax import lax

D = 512
HEADS = 16
LV = 2
WIN_LAT = 6
WIN_LON = 12
NLAT = 192
NLON = 384


def draw_qkv_weight(key, part):
    key = jax.random.fold_in(key, 11)
    base = jnp.clip(jax.random.normal(key, (D, 3 * D), jnp.float32), -4.0, 4.0)
    return (base * D ** (-0.5)).astype(jnp.bfloat16)


def spiked(array, own_key, source, target, blocks, factor):
    def block_of(dim):
        return (jnp.arange(array.shape[dim]) // (array.shape[dim] // blocks)).reshape((-1,) + (1,) * (array.ndim - 1 - dim))

    first = jax.random.permutation(own_key, blocks)[block_of(target)]
    second = (block_of(target) + blocks // 2) % blocks
    return jnp.where((block_of(source) == first) | (block_of(source) == second), factor * array, array)


def steps_of(own_key, dims, pieces, low, top_value):
    def one(position, parts):
        draws = jax.random.uniform(jax.random.fold_in(jax.random.fold_in(own_key, 6), position), (parts,), jnp.float32, low / len(pieces), top_value / len(pieces))
        return jnp.repeat(jnp.exp(draws), dims[position] // parts).reshape((-1,) + (1,) * (len(dims) - position - 1))

    loudness = one(*pieces[0])
    for cut in pieces[1:]:
        loudness = loudness * one(*cut)
    return loudness


def normal_values(key, shape, scale, reach, split=(), held_as=jnp.bfloat16):
    loudness = steps_of(key, shape, split, -0.22, 0.18) if split else 1.0
    entries = jax.random.normal(key, shape, jnp.float32) * scale * loudness
    return jnp.minimum(jnp.maximum(entries, -reach), reach).astype(held_as)


def noise_with(key, shape, scale, limit, cuts, heavy, kind=jnp.bfloat16):
    values = scale * jax.random.normal(key, shape, jnp.float32)
    if cuts:
        values = values * steps_of(key, shape, cuts, -0.22, 0.18)
    return jnp.clip(spiked(values, jax.random.fold_in(key, 3), *heavy), -limit, limit).astype(kind)


def setup_inputs(seed: int = 0) -> dict:
    keys = jax.random.split(jax.random.key(seed), 5)
    fields = noise_with(keys[0], (LV, NLAT, NLON, D), 1.0, 6.0, ((1, 8), (2, 16)), (2, 3, 16, 2.0))
    cotangent = normal_values(keys[1], (LV, NLAT, NLON, D), 1.0, 6.0, ((1, 8), (2, 16)))
    qkv_weight = draw_qkv_weight(jax.random.fold_in(keys[4], 71), 0)
    out_weight = normal_values(keys[3], (D, D), D ** -0.5, 0.25)
    return dict(fields=fields, cotangent=cotangent, qkv_weight=qkv_weight, out_weight=out_weight)


def normalize(values):
    center = lax.optimization_barrier(jnp.mean(values, axis=-1, keepdims=True))
    centred = values - center
    spread = lax.optimization_barrier(jnp.mean(centred * centred, axis=-1, keepdims=True))
    return centred * lax.rsqrt(spread + 1e-05)

def attend(projected, groups):
    wincount, tokens_win, triple = projected.shape
    width = triple // 3
    head_size = width // HEADS
    queries = projected[..., :width].reshape(wincount, tokens_win, HEADS, head_size).astype(jnp.float32)
    keyset = projected[..., width:2 * width].reshape(wincount, tokens_win, HEADS, head_size).astype(jnp.float32)
    valueset = projected[..., 2 * width:].reshape(wincount, tokens_win, HEADS, head_size).astype(jnp.float32)
    scores = jnp.einsum('wqhe,wkhe->whqk', queries, keyset) * head_size ** (-0.5)
    allowed = (groups[:, :, None] == groups[:, None, :])[:, None]
    scores = jnp.where(allowed, scores, -1000000000.0)
    highest = lax.optimization_barrier(jnp.max(scores, axis=-1, keepdims=True))
    raised = jnp.exp(scores - highest)
    soft_weights = (raised / lax.optimization_barrier(jnp.sum(raised, axis=-1, keepdims=True))).astype(jnp.bfloat16)
    mixture = jnp.einsum('whqk,wkhe->wqhe', soft_weights.astype(jnp.float32), valueset)
    return mixture.reshape(wincount, tokens_win, width).astype(jnp.bfloat16)

def to_windows(grid):
    levels, lat_cells, lon_cells, channels = grid.shape
    shaped = grid.reshape(levels, lat_cells // WIN_LAT, WIN_LAT, lon_cells // WIN_LON, WIN_LON, channels)
    shaped = shaped.transpose(1, 3, 0, 2, 4, 5)
    return shaped.reshape(lat_cells // WIN_LAT * (lon_cells // WIN_LON), levels * WIN_LAT * WIN_LON, channels)

def from_windows(windows, levels, lat_cells, lon_cells):
    channels = windows.shape[-1]
    shaped = windows.reshape(lat_cells // WIN_LAT, lon_cells // WIN_LON, levels, WIN_LAT, WIN_LON, channels)
    shaped = shaped.transpose(2, 0, 3, 1, 4, 5)
    return shaped.reshape(levels, lat_cells, lon_cells, channels)

def reference(fields, cotangent, qkv_weight, out_weight):
    shift_lat = WIN_LAT // 2
    shift_lon = WIN_LON // 2
    rolled = jnp.roll(fields, (-shift_lat, -shift_lon), axis=(1, 2))
    windows = to_windows(rolled)
    wincount, tokens_win, width = windows.shape
    tokens_flat = windows.reshape(-1, width)
    lat_rows = jnp.arange(NLAT, dtype=jnp.int32)
    group_rows = (lat_rows >= NLAT - shift_lat).astype(jnp.int32)
    group_grid = jnp.broadcast_to(group_rows[None, :, None, None], (LV, NLAT, NLON, 1)).astype(jnp.int32)
    groups = to_windows(group_grid)[..., 0]
    norm_core, norm_back = jax.vjp(normalize, tokens_flat.astype(jnp.float32))
    normed = norm_core.astype(jnp.bfloat16)
    projected = jnp.dot(normed, qkv_weight, preferred_element_type=jnp.float32).astype(jnp.bfloat16)
    row_windows = NLON // WIN_LON

    def attend_all(values):
        shaped = values.reshape(wincount // row_windows, row_windows, tokens_win, 3 * width)
        shaped_groups = groups.reshape(wincount // row_windows, row_windows, tokens_win)
        result = lax.map(lambda operands: attend(operands[0], operands[1]), (shaped, shaped_groups))
        return result.reshape(wincount, tokens_win, width)
    mixture, attend_back = jax.vjp(attend_all, projected.reshape(wincount, tokens_win, 3 * width))
    attended = mixture.reshape(-1, width)
    output_rows = (tokens_flat.astype(jnp.float32) + jnp.dot(attended, out_weight, preferred_element_type=jnp.float32)).astype(jnp.bfloat16)
    output_grid = from_windows(output_rows.reshape(wincount, tokens_win, width), LV, NLAT, NLON)
    output_field = jnp.roll(output_grid, (shift_lat, shift_lon), axis=(1, 2))
    grad_rolled = jnp.roll(cotangent, (-shift_lat, -shift_lon), axis=(1, 2))
    grad_rows = to_windows(grad_rolled).reshape(-1, width)
    out_grad = lax.dot_general(attended, grad_rows, (((0,), (0,)), ((), ())), preferred_element_type=jnp.float32)
    grad_attended = lax.dot_general(grad_rows, out_weight, (((1,), (1,)), ((), ())), preferred_element_type=jnp.float32).astype(jnp.bfloat16)
    grad_projected = attend_back(grad_attended.reshape(wincount, tokens_win, width))[0].reshape(-1, 3 * width)
    qkv_grad = lax.dot_general(normed, grad_projected, (((0,), (0,)), ((), ())), preferred_element_type=jnp.float32)
    grad_normed = lax.dot_general(grad_projected, qkv_weight, (((1,), (1,)), ((), ())), preferred_element_type=jnp.float32)
    grad_centred = norm_back(grad_normed)[0]
    grad_tokens = (grad_rows.astype(jnp.float32) + grad_centred).astype(jnp.bfloat16)
    grad_grid = from_windows(grad_tokens.reshape(wincount, tokens_win, width), LV, NLAT, NLON)
    field_grad = jnp.roll(grad_grid, (shift_lat, shift_lon), axis=(1, 2))
    return (output_field, field_grad, qkv_grad, out_grad)
```

```python
import functools, math
import jax
import jax.numpy as jnp
from jax import lax
from jax.experimental import pallas as pl
from jax.experimental.pallas import tpu as pltpu
from jax.sharding import PartitionSpec as P

D = 512
HEADS = 16
HD = 32
T = 144
NW = 8
TOK = NW * T
F32 = jnp.float32
BF = jnp.bfloat16
EPS = 1e-5
SCALE = HD ** -0.5
LOG2E = math.log2(math.e)
LN2 = math.log(2.0)


def nt(a, b):
    return lax.dot_general(a, b, (((1,), (1,)), ((), ())), preferred_element_type=F32)


def nn(a, b):
    return lax.dot_general(a, b, (((1,), (0,)), ((), ())), preferred_element_type=F32)


def tn(a, b):
    return lax.dot_general(a, b, (((0,), (0,)), ((), ())), preferred_element_type=F32)


def norm_stats(x):
    mean = jnp.sum(x, axis=-1, keepdims=True) * (1.0 / D)
    xc = x - mean
    var = jnp.sum(xc * xc, axis=-1, keepdims=True) * (1.0 / D)
    return xc, lax.rsqrt(var + EPS)


def heads_apart(a):
    lane = lax.broadcasted_iota(jnp.int32, (1, 128), 1) // HD
    zero = jnp.zeros((T, 128), BF)
    parts = []
    for h in range(8):
        mask = jnp.where(lane == h % 4, 1.0, 0.0).astype(BF)
        own = a[:, 128 * (h // 4) : 128 * (h // 4) + 128] * mask
        parts.append(jnp.concatenate([own, zero] if h < 4 else [zero, own], axis=1))
    return jnp.concatenate(parts, axis=0)


def heads_together(a):
    lane = lax.broadcasted_iota(jnp.int32, (1, 128), 1) // HD
    halves = []
    for c in range(2):
        cols = slice(128 * c, 128 * c + 128)
        own = a[T * 4 * c : T * 4 * c + T, cols]
        for h in range(1, 4):
            at = T * (4 * c + h)
            own = jnp.where(lane == h, a[at : at + T, cols], own)
        halves.append(own)
    return jnp.concatenate(halves, axis=1)


def attention(w, big, q_s, k_s, v_s, do_s, o_s, dp_s):
    rows = pl.ds(pl.multiple_of(w * T, 16), T)
    half = T // 2
    query = lax.broadcasted_iota(jnp.int32, (1, 8 * T), 1) % T
    pen0 = jnp.where(query >= half, big, 0.0)
    pen1 = jnp.where(query < half, big, 0.0)
    for g in range(2):
        qg = q_s[g, rows, :]
        kg = k_s[g, rows, :]
        vg = v_s[g, rows, :]
        qm = heads_apart(qg)
        dom = heads_apart(do_s[g, rows, :])
        st = nt(kg, qm)
        dpt = nt(vg, dom)
        top = jnp.maximum(
            jnp.max(st[:half], axis=0, keepdims=True) - pen0, jnp.max(st[half:], axis=0, keepdims=True) - pen1
        )
        e = jnp.concatenate([jnp.exp2(st[:half] - (top + pen0)), jnp.exp2(st[half:] - (top + pen1))], axis=0)
        p = e * (1.0 / jnp.sum(e, axis=0, keepdims=True))
        pb = p.astype(BF)
        ds = (p * (dpt - jnp.sum(p * dpt, axis=0, keepdims=True))).astype(BF)
        cols = slice(256 * g, 256 * g + 256)
        o_s[rows, cols] = heads_together(tn(pb, vg)).astype(BF)
        dp_s[rows, 1024 + 256 * g : 1280 + 256 * g] = nn(pb, dom).astype(BF)
        dp_s[rows, 512 + 256 * g : 768 + 256 * g] = (nn(ds, qm) * LN2).astype(BF)
        dp_s[rows, cols] = (heads_together(tn(ds, kg)) * SCALE).astype(BF)


MESH = pl.DeviceIdType.MESH
E_AT, S_AT, C_AT, MSG = 0, 256, 368, 416
PARTS = ((E_AT, 256), (S_AT, 112), (C_AT, 48))
FREE = 3 * T


def window_of(i, j):
    if i < 3:
        return i + 3 * j
    return 6 + j


def neighbours(by):
    lon, lat = lax.axis_index("lon"), lax.axis_index("lat")
    nlon, nlat = lax.axis_size("lon"), lax.axis_size("lat")
    lon2, lat2 = lax.rem(lon + by + nlon, nlon), lax.rem(lat + by + nlat, nlat)
    return [(lon2, lat), (lon, lat2), (lon2, lat2)]


def halo_copies(which, send, recv, send_sem, recv_sem, to):
    return [
        pltpu.make_async_remote_copy(
            src_ref=send.at[which, pl.ds(at, rows)],
            dst_ref=recv.at[which, pl.ds(at, rows)],
            send_sem=send_sem.at[which, n],
            recv_sem=recv_sem.at[which, n],
            device_id=peer,
            device_id_type=MESH,
        )
        for n, ((at, rows), peer) in enumerate(zip(PARTS, to))
    ]


def kernel(
    f_ref, c_ref, w_ref, wo_ref, of_ref, df_ref, qg_ref, og_ref,
    wide, rows_s, pack, send_in, recv_in, send_out, recv_out, in_send, in_recv, out_send, out_recv,
    xw, gw, xn_s, q_s, k_s, v_s, do_s, o_s, dp_s, wt_s, wot_s,
    wg, r0, t0, r1x, r1z, t1x, t1z, r2, tc, t3f, t3, r3, rs_send, rs_recv,
):
    lon, lat = lax.axis_index("lon"), lax.axis_index("lat")
    core, x, zh = lax.rem(lon, 2), lax.rem(lon // 2, 4), lon // 8
    y, zl = lax.rem(lat, 4), lat // 4
    z = zh * 2 + zl

    def at(zh_, x_, core_, zl_, y_):
        return ((zh_ * 4 + x_) * 2 + core_, zl_ * 4 + y_)

    def step(v, d):
        return lax.rem(v + d, 4)

    partner = at(zh, x, 1 - core, zl, y)
    along_x = [at(zh, step(x, d), core, zl, y) for d in (1, 2, 3)]
    along_z = [at(step(z, d) // 2, x, core, lax.rem(step(z, d), 2), y) for d in (1, 2, 3)]
    along_y = [at(zh, x, core, zl, step(y, d)) for d in (1, 2, 3)]
    ahead, behind = neighbours(1), neighbours(-1)
    peers = ahead + behind + [partner] + along_x + along_z + along_y
    barrier = pltpu.get_barrier_semaphore()
    for peer in peers:
        pl.semaphore_signal(barrier, inc=1, device_id=peer, device_id_type=MESH)

    def rdma(src, dst, n, peer):
        copy = pltpu.make_async_remote_copy(
            src_ref=src, dst_ref=dst, send_sem=rs_send.at[n], recv_sem=rs_recv.at[n],
            device_id=peer, device_id_type=MESH,
        )
        copy.start()
        return copy

    halo_in = []
    for which, src in enumerate((f_ref, c_ref)):
        for l in range(2):
            for a in range(24):
                i, ar = (a - 3) // 6, (a - 3) % 6
                if a < 3:
                    row = src[l, a].astype(F32)
                    n = l * 3 + a
                    pack[S_AT + n * 12 : S_AT + n * 12 + 12] = row[6:18]
                    pack[S_AT + 72 + n * 6 : S_AT + 72 + n * 6 + 6] = row[18:24]
                    pack[C_AT + n * 6 : C_AT + n * 6 + 6] = row[0:6]
                else:
                    row = src[l, a, 0:16].astype(F32)
                    n = l * 6 + ar if i < 3 else l * 3 + ar
                    pack[E_AT + 72 * i + n * 6 : E_AT + 72 * i + n * 6 + 6] = row[0:6]
        send_in[which] = pack[...].astype(BF)
        if which == 0:
            pl.semaphore_wait(barrier, len(peers))
        halo_in.append(halo_copies(which, send_in, recv_in, in_send, in_recv, behind))
        for copy in halo_in[-1]:
            copy.start()

    for which, src in enumerate((f_ref, c_ref)):
        for l in range(2):
            for a in range(3, 24):
                i, ar = (a - 3) // 6, (a - 3) % 6
                row = src[l, a].astype(F32)
                n = l * 6 + ar if i < 3 else l * 3 + ar
                wide[which, window_of(i, 0), n * 12 : n * 12 + 12] = row[6:18]
                wide[which, window_of(i, 1), n * 6 : n * 6 + 6] = row[18:24]
    wt_s[...] = w_ref[...].T
    wot_s[...] = wo_ref[...].T

    def project(first, count):
        rows = slice(first * T, (first + count) * T)
        for w in range(first, first + count):
            at_ = slice(w * T, w * T + T)
            gw[at_] = wide[1, w].astype(BF)
            xv = wide[0, w]
            xw[at_] = xv.astype(BF)
            xc, rstd = norm_stats(xv)
            xn_s[at_] = (xc * rstd).astype(BF)
        for part, (dst, scale) in enumerate(((q_s, SCALE * LOG2E), (k_s, None), (v_s, None))):
            for n in range(2):
                res = nn(xn_s[rows], w_ref[:, 512 * part + 256 * n : 512 * part + 256 * n + 256])
                if scale is not None:
                    res = res * scale
                dst[n, rows] = res.astype(BF)
        for n in range(2):
            do_s[n, rows] = nn(gw[rows], wot_s[:, 256 * n : 256 * n + 256]).astype(BF)

    last = jnp.where(lat == lax.axis_size("lat") - 1, 1e9, 0.0)

    def attend(first, count):
        def window(w, _):
            big = jnp.where(w >= NW - 2, last, 0.0).astype(F32)
            attention(w, big, q_s, k_s, v_s, do_s, o_s, dp_s)
            return 0

        lax.fori_loop(first, first + count, window, 0)

    def finish_out(first, count):
        for w in range(first, first + count):
            at_ = slice(w * T, w * T + T)
            wide[0, w] = xw[at_].astype(F32) + nn(o_s[at_], wo_ref[...])

    def finish_grad(first, count):
        for w in range(first, first + count):
            at_ = slice(w * T, w * T + T)
            gn = nn(dp_s[at_], wt_s[...])
            xc, rstd = norm_stats(xw[at_].astype(F32))
            xh = xc * rstd
            m1 = jnp.sum(gn, axis=-1, keepdims=True) * (1.0 / D)
            m2 = jnp.sum(gn * xh, axis=-1, keepdims=True) * (1.0 / D)
            wide[1, w] = gw[at_].astype(F32) + rstd * (gn - m1 - xh * m2)

    project(0, 3)
    attend(0, 1)

    for which in range(2):
        for copy in halo_in[which]:
            copy.wait()
        pack[...] = recv_in[which].astype(F32)
        for i in range(3):
            wide[which, 3 + i, 72:144] = pack[E_AT + 72 * i : E_AT + 72 * i + 72]
        wide[which, 7, 36:72] = pack[E_AT + 216 : E_AT + 252]
        wide[which, 6, 72:144] = pack[S_AT : S_AT + 72]
        wide[which, 7, 72:108] = pack[S_AT + 72 : S_AT + 108]
        wide[which, 7, 108:144] = pack[C_AT : C_AT + 36]

    project(3, 5)
    attend(3, 5)

    halo_out = []
    for which, finish in enumerate((finish_out, finish_grad)):
        finish(3, 5)
        for i in range(3):
            pack[E_AT + 72 * i : E_AT + 72 * i + 72] = wide[which, 3 + i, 72:144]
        pack[E_AT + 216 : E_AT + 252] = wide[which, 7, 36:72]
        pack[S_AT : S_AT + 72] = wide[which, 6, 72:144]
        pack[S_AT + 72 : S_AT + 108] = wide[which, 7, 72:108]
        pack[C_AT : C_AT + 36] = wide[which, 7, 108:144]
        send_out[which] = pack[...].astype(BF)
        halo_out.append(halo_copies(which, send_out, recv_out, out_send, out_recv, ahead))
        for copy in halo_out[-1]:
            copy.start()

    attend(1, 2)

    def term(b):
        if b < 3:
            res = tn(xn_s[...], dp_s[:, 512 * b : 512 * b + 512])
        else:
            res = tn(o_s[...], gw[...])
        wg[b] = res.astype(BF).reshape(2, 4, 2, 2, 16, 512)
        return rdma(wg.at[b, :, :, 1 - core], r0.at[b], b, partner)

    def first_axis(b):
        copies = []
        for a in range(2):
            for k in range(4):
                t0[b, a, k] = (wg[b, a, k, core].astype(F32) + r0[b, a, k].astype(F32)).astype(BF)
        for d in (1, 2, 3):
            xd, zd = step(x, d), step(z, d)
            if b % 2 == 0:
                src, to = t0.at[b, :, xd], along_x[d - 1]
            else:
                src, to = t0.at[b, zd // 2, :, lax.rem(zd, 2)], along_z[d - 1]
            dst = (r1z if b % 2 else r1x).at[b // 2, d - 1]
            copies.append(rdma(src, dst, 4 + 3 * b + d - 1, to))
        return copies

    core_copies = [term(0), term(1)]
    stage1 = []
    core_copies[0].wait()
    stage1.append(first_axis(0))
    core_copies.append(term(2))
    core_copies[1].wait()
    stage1.append(first_axis(1))
    core_copies.append(term(3))
    core_copies[2].wait()
    stage1.append(first_axis(2))
    finish_out(0, 3)
    core_copies[3].wait()
    stage1.append(first_axis(3))
    finish_grad(0, 3)

    def second_axis(b):
        for copy in stage1[b]:
            copy.wait()
        copies = []
        got, t1 = (r1z, t1z) if b % 2 else (r1x, t1x)
        if b % 2 == 0:
            acc = t0[b, :, x].astype(F32)
        else:
            acc = t0[b, zh, :, zl].astype(F32)
        for d in range(3):
            acc = acc + got[b // 2, d].astype(F32)
        t1[b // 2] = acc.astype(BF)
        for d in (1, 2, 3):
            xd, zd = step(x, d), step(z, d)
            if b % 2 == 0:
                src, to = t1.at[b // 2, zd // 2, lax.rem(zd, 2)], along_z[d - 1]
            else:
                src, to = t1.at[b // 2, xd], along_x[d - 1]
            copies.append(rdma(src, r2.at[b, d - 1], 16 + 3 * b + d - 1, to))
        return copies

    def assemble(which, dst):
        for copy in halo_out[which]:
            copy.wait()
        pack[...] = recv_out[which].astype(F32)
        for l in range(2):
            for a in range(24):
                i, ar = (a - 3) // 6, (a - 3) % 6
                at_ = l * 24 + a
                if a < 3:
                    n = l * 3 + a
                    rows_s[at_, 6:18] = pack[S_AT + n * 12 : S_AT + n * 12 + 12]
                    rows_s[at_, 18:24] = pack[S_AT + 72 + n * 6 : S_AT + 72 + n * 6 + 6]
                    rows_s[at_, 0:6] = pack[C_AT + n * 6 : C_AT + n * 6 + 6]
                else:
                    n = l * 6 + ar if i < 3 else l * 3 + ar
                    rows_s[at_, 0:6] = pack[E_AT + 72 * i + n * 6 : E_AT + 72 * i + n * 6 + 6]
                    rows_s[at_, 6:18] = wide[which, window_of(i, 0), n * 12 : n * 12 + 12]
                    rows_s[at_, 18:24] = wide[which, window_of(i, 1), n * 6 : n * 6 + 6]
                dst[l, a] = rows_s[at_].astype(BF)

    stage2 = [second_axis(0), second_axis(1)]
    assemble(0, of_ref)
    stage2 += [second_axis(2), second_axis(3)]
    assemble(1, df_ref)

    for b in range(4):
        for copy in stage2[b]:
            copy.wait()
        if b % 2 == 0:
            acc = t1x[b // 2, zh, zl].astype(F32)
        else:
            acc = t1z[b // 2, x].astype(F32)
        for d in range(3):
            acc = acc + r2[b, d].astype(F32)
        tc[...] = acc
        for k in range(4):
            t3f[k, 4 * b : 4 * b + 4] = tc[4 * k : 4 * k + 4]
    t3[...] = t3f[...].astype(BF)
    stage3 = [rdma(t3.at[step(y, d)], r3.at[d - 1], 28 + d - 1, along_y[d - 1]) for d in (1, 2, 3)]
    for copy in stage3:
        copy.wait()
    acc = t3f[y]
    for d in range(3):
        acc = acc + r3[d].astype(F32)
    tc[...] = acc
    for b in range(3):
        qg_ref[:, 512 * b : 512 * b + 512] = tc[4 * b : 4 * b + 4]
    og_ref[...] = tc[12:16]


def shards(fields, cotangent, qkv_weight, out_weight):
    vm = pl.BlockSpec(memory_space=pltpu.VMEM)
    return tuple(
        pl.pallas_call(
            kernel,
            out_shape=[
                jax.ShapeDtypeStruct((2, 24, 24, D), BF),
                jax.ShapeDtypeStruct((2, 24, 24, D), BF),
                jax.ShapeDtypeStruct((4, 3 * D), F32),
                jax.ShapeDtypeStruct((4, D), F32),
            ],
            in_specs=[vm] * 4,
            out_specs=[vm] * 4,
            scratch_shapes=[
                pltpu.VMEM((2, NW, T, D), F32),
                pltpu.VMEM((48, 24, D), F32),
                pltpu.VMEM((MSG, D), F32),
            ]
            + [pltpu.VMEM((2, MSG, D), BF)] * 4
            + [pltpu.SemaphoreType.DMA((2, 3))] * 4
            + [pltpu.VMEM((TOK, D), BF)] * 3
            + [pltpu.VMEM((2, TOK, 256), BF)] * 4
            + [
                pltpu.VMEM((TOK, D), BF),
                pltpu.VMEM((TOK, 3 * D), BF),
                pltpu.VMEM((3 * D, D), BF),
                pltpu.VMEM((D, D), BF),
                pltpu.VMEM((4, 2, 4, 2, 2, 16, 512), BF),
                pltpu.VMEM((4, 2, 4, 2, 16, 512), BF),
                pltpu.VMEM((4, 2, 4, 2, 16, 512), BF),
                pltpu.VMEM((2, 3, 2, 2, 16, 512), BF),
                pltpu.VMEM((2, 3, 4, 16, 512), BF),
                pltpu.VMEM((2, 2, 2, 16, 512), BF),
                pltpu.VMEM((2, 4, 16, 512), BF),
                pltpu.VMEM((4, 3, 16, 512), BF),
                pltpu.VMEM((16, D), F32),
                pltpu.VMEM((4, 16, D), F32),
                pltpu.VMEM((4, 16, D), BF),
                pltpu.VMEM((3, 16, D), BF),
                pltpu.SemaphoreType.DMA((31,)),
                pltpu.SemaphoreType.DMA((31,)),
            ],
            compiler_params=pltpu.CompilerParams(
                collective_id=0, has_side_effects=True, vmem_limit_bytes=58 * 1024 * 1024
            ),
            cost_estimate=pl.CostEstimate(flops=10 * 10**9, bytes_accessed=8 * 10**6, transcendentals=3 * 10**6),
        )(fields, cotangent, qkv_weight, out_weight)
    )


def solution(mesh):
    placed = (P(None, "lat", "lon", None), P(None, "lat", "lon", None), P(), P())
    return jax.shard_map(
        shards,
        mesh=mesh,
        in_specs=placed,
        out_specs=(
            P(None, "lat", "lon", None),
            P(None, "lat", "lon", None),
            P(("lon", "lat"), None),
            P(("lon", "lat"), None),
        ),
        check_vma=False,
    )
```

```python
import functools, math
import jax
import jax.numpy as jnp
from jax import lax
from jax.experimental import pallas as pl
from jax.experimental.pallas import tpu as pltpu
from jax.sharding import PartitionSpec as P

D = 512
HEADS = 16
HD = 32
T = 144
NW = 8
TOK = NW * T
F32 = jnp.float32
BF = jnp.bfloat16
EPS = 1e-5
SCALE = HD ** -0.5
LOG2E = math.log2(math.e)
LN2 = math.log(2.0)


def nt(a, b):
    return lax.dot_general(a, b, (((1,), (1,)), ((), ())), preferred_element_type=F32)


def nn(a, b):
    return lax.dot_general(a, b, (((1,), (0,)), ((), ())), preferred_element_type=F32)


def tn(a, b):
    return lax.dot_general(a, b, (((0,), (0,)), ((), ())), preferred_element_type=F32)


def norm_stats(x):
    mean = jnp.sum(x, axis=-1, keepdims=True) * (1.0 / D)
    xc = x - mean
    var = jnp.sum(xc * xc, axis=-1, keepdims=True) * (1.0 / D)
    return xc, lax.rsqrt(var + EPS)


def heads_apart(a):
    lane = lax.broadcasted_iota(jnp.int32, (1, 128), 1) // HD
    zero = jnp.zeros((T, 128), BF)
    parts = []
    for h in range(8):
        mask = jnp.where(lane == h % 4, 1.0, 0.0).astype(BF)
        own = a[:, 128 * (h // 4) : 128 * (h // 4) + 128] * mask
        parts.append(jnp.concatenate([own, zero] if h < 4 else [zero, own], axis=1))
    return jnp.concatenate(parts, axis=0)


def heads_together(a):
    lane = lax.broadcasted_iota(jnp.int32, (1, 128), 1) // HD
    halves = []
    for c in range(2):
        cols = slice(128 * c, 128 * c + 128)
        own = a[T * 4 * c : T * 4 * c + T, cols]
        for h in range(1, 4):
            at = T * (4 * c + h)
            own = jnp.where(lane == h, a[at : at + T, cols], own)
        halves.append(own)
    return jnp.concatenate(halves, axis=1)


def attention(w, big, q_s, k_s, v_s, p_s, o_s):
    rows = pl.ds(pl.multiple_of(w * T, 16), T)
    half = T // 2
    query = lax.broadcasted_iota(jnp.int32, (1, 8 * T), 1) % T
    pen0 = jnp.where(query >= half, big, 0.0)
    pen1 = jnp.where(query < half, big, 0.0)
    for g in range(2):
        st = nt(k_s[g, rows, :], heads_apart(q_s[g, rows, :]))
        top = jnp.maximum(
            jnp.max(st[:half], axis=0, keepdims=True) - pen0, jnp.max(st[half:], axis=0, keepdims=True) - pen1
        )
        e = jnp.concatenate([jnp.exp2(st[:half] - (top + pen0)), jnp.exp2(st[half:] - (top + pen1))], axis=0)
        pb = (e * (1.0 / jnp.sum(e, axis=0, keepdims=True))).astype(BF)
        p_s[w, g] = pb
        o_s[rows, 256 * g : 256 * g + 256] = heads_together(tn(pb, v_s[g, rows, :])).astype(BF)


def attention_back(w, q_s, k_s, v_s, p_s, do_s, dp_s):
    rows = pl.ds(pl.multiple_of(w * T, 16), T)
    for g in range(2):
        kg = k_s[g, rows, :]
        qm = heads_apart(q_s[g, rows, :])
        dom = heads_apart(do_s[g, rows, :])
        dpt = nt(v_s[g, rows, :], dom)
        pb = p_s[w, g]
        p = pb.astype(F32)
        ds = (p * (dpt - jnp.sum(p * dpt, axis=0, keepdims=True))).astype(BF)
        dp_s[rows, 1024 + 256 * g : 1280 + 256 * g] = nn(pb, dom).astype(BF)
        dp_s[rows, 512 + 256 * g : 768 + 256 * g] = (nn(ds, qm) * LN2).astype(BF)
        dp_s[rows, 256 * g : 256 * g + 256] = (heads_together(tn(ds, kg)) * SCALE).astype(BF)


MESH = pl.DeviceIdType.MESH
E_AT, S_AT, C_AT, MSG = 0, 256, 368, 416
PARTS = ((E_AT, 256), (S_AT, 112), (C_AT, 48))
FREE = 3 * T


def window_of(i, j):
    if i < 3:
        return i + 3 * j
    return 6 + j


def neighbours(by):
    lon, lat = lax.axis_index("lon"), lax.axis_index("lat")
    nlon, nlat = lax.axis_size("lon"), lax.axis_size("lat")
    lon2, lat2 = lax.rem(lon + by + nlon, nlon), lax.rem(lat + by + nlat, nlat)
    return [(lon2, lat), (lon, lat2), (lon2, lat2)]


def halo_copies(which, send, recv, send_sem, recv_sem, to):
    return [
        pltpu.make_async_remote_copy(
            src_ref=send.at[which, pl.ds(at, rows)],
            dst_ref=recv.at[which, pl.ds(at, rows)],
            send_sem=send_sem.at[which, n],
            recv_sem=recv_sem.at[which, n],
            device_id=peer,
            device_id_type=MESH,
        )
        for n, ((at, rows), peer) in enumerate(zip(PARTS, to))
    ]


def kernel(
    f_any, c_any, w_any, wo_any, of_ref, df_ref, qg_ref, og_ref,
    f_ref, c_ref, w_ref, wo_ref, load_sem,
    wide, rows_s, pack, send_in, recv_in, send_out, recv_out, in_send, in_recv, out_send, out_recv,
    xw, gw, xn_s, q_s, k_s, v_s, do_s, o_s, dp_s, p_s, wt_s, wot_s,
    wg, r0, cut, t0, r1, t1, r2, t2, r3, t3, rs_send, rs_recv,
):
    lon, lat = lax.axis_index("lon"), lax.axis_index("lat")
    core, x, zh = lax.rem(lon, 2), lax.rem(lon // 2, 4), lon // 8
    y, zl = lax.rem(lat, 4), lat // 4
    z = zh * 2 + zl

    def at(zh_, x_, core_, zl_, y_):
        return ((zh_ * 4 + x_) * 2 + core_, zl_ * 4 + y_)

    def step(v, d):
        return lax.rem(v + d, 4)

    partner = at(zh, x, 1 - core, zl, y)
    position = {"x": x, "y": y, "z": z}
    along = {
        "x": [at(zh, step(x, d), core, zl, y) for d in (1, 2, 3)],
        "y": [at(zh, x, core, zl, step(y, d)) for d in (1, 2, 3)],
        "z": [at(step(z, d) // 2, x, core, lax.rem(step(z, d), 2), y) for d in (1, 2, 3)],
    }
    ahead, behind = neighbours(1), neighbours(-1)
    peers = ahead + behind + [partner] + along["x"] + along["y"] + along["z"]
    barrier = pltpu.get_barrier_semaphore()
    for peer in peers:
        pl.semaphore_signal(barrier, inc=1, device_id=peer, device_id_type=MESH)
    loads = [
        pltpu.make_async_copy(src, dst, load_sem.at[n])
        for n, (src, dst) in enumerate(((f_any, f_ref), (c_any, c_ref), (w_any, w_ref), (wo_any, wo_ref)))
    ]
    for load in loads:
        load.start()

    halo_in = []

    def pack_in(which, src):
        loads[which].wait()
        for l in range(2):
            for a in range(24):
                i, ar = (a - 3) // 6, (a - 3) % 6
                if a < 3:
                    row = src[l, a].astype(F32)
                    n = l * 3 + a
                    pack[S_AT + n * 12 : S_AT + n * 12 + 12] = row[6:18]
                    pack[S_AT + 72 + n * 6 : S_AT + 72 + n * 6 + 6] = row[18:24]
                    pack[C_AT + n * 6 : C_AT + n * 6 + 6] = row[0:6]
                else:
                    row = src[l, a, 0:16].astype(F32)
                    n = l * 6 + ar if i < 3 else l * 3 + ar
                    pack[E_AT + 72 * i + n * 6 : E_AT + 72 * i + n * 6 + 6] = row[0:6]
        send_in[which] = pack[...].astype(BF)

    def send(which):
        halo_in.append(halo_copies(which, send_in, recv_in, in_send, in_recv, behind))
        for copy in halo_in[-1]:
            copy.start()

    def own(which, src):
        for l in range(2):
            for a in range(3, 24):
                i, ar = (a - 3) // 6, (a - 3) % 6
                row = src[l, a].astype(F32)
                n = l * 6 + ar if i < 3 else l * 3 + ar
                wide[which, window_of(i, 0), n * 12 : n * 12 + 12] = row[6:18]
                wide[which, window_of(i, 1), n * 6 : n * 6 + 6] = row[18:24]

    pack_in(0, f_ref)
    own(0, f_ref)
    pl.semaphore_wait(barrier, len(peers))
    send(0)
    pack_in(1, c_ref)
    own(1, c_ref)
    loads[2].wait()
    loads[3].wait()
    wt_s[...] = w_ref[...].T
    wot_s[...] = wo_ref[...].T

    def project(first, count):
        rows = slice(first * T, (first + count) * T)
        for w in range(first, first + count):
            at_ = slice(w * T, w * T + T)
            xv = wide[0, w]
            xw[at_] = xv.astype(BF)
            xc, rstd = norm_stats(xv)
            xn_s[at_] = (xc * rstd).astype(BF)
        for part, (dst, scale) in enumerate(((q_s, SCALE * LOG2E), (k_s, None), (v_s, None))):
            for n in range(2):
                res = nn(xn_s[rows], w_ref[:, 512 * part + 256 * n : 512 * part + 256 * n + 256])
                if scale is not None:
                    res = res * scale
                dst[n, rows] = res.astype(BF)

    last = jnp.where(lat == lax.axis_size("lat") - 1, 1e9, 0.0)

    def attend(first, count):
        def window(w, _):
            big = jnp.where(w >= NW - 2, last, 0.0).astype(F32)
            attention(w, big, q_s, k_s, v_s, p_s, o_s)
            return 0

        lax.fori_loop(first, first + count, window, 0)

    def attend_back(first, count):
        def window(w, _):
            attention_back(w, q_s, k_s, v_s, p_s, do_s, dp_s)
            return 0

        lax.fori_loop(first, first + count, window, 0)

    def finish_out(first, count):
        for w in range(first, first + count):
            at_ = slice(w * T, w * T + T)
            wide[0, w] = xw[at_].astype(F32) + nn(o_s[at_], wo_ref[...])

    def finish_grad(first, count):
        for w in range(first, first + count):
            at_ = slice(w * T, w * T + T)
            gn = nn(dp_s[at_], wt_s[...])
            xc, rstd = norm_stats(xw[at_].astype(F32))
            xh = xc * rstd
            m1 = jnp.sum(gn, axis=-1, keepdims=True) * (1.0 / D)
            m2 = jnp.sum(gn * xh, axis=-1, keepdims=True) * (1.0 / D)
            wide[1, w] = gw[at_].astype(F32) + rstd * (gn - m1 - xh * m2)

    def halo_arrived(which):
        for copy in halo_in[which]:
            copy.wait()
        pack[...] = recv_in[which].astype(F32)
        for i in range(3):
            wide[which, 3 + i, 72:144] = pack[E_AT + 72 * i : E_AT + 72 * i + 72]
        wide[which, 7, 36:72] = pack[E_AT + 216 : E_AT + 252]
        wide[which, 6, 72:144] = pack[S_AT : S_AT + 72]
        wide[which, 7, 72:108] = pack[S_AT + 72 : S_AT + 108]
        wide[which, 7, 108:144] = pack[C_AT : C_AT + 36]

    halo_out = []

    def send_back(which):
        for i in range(3):
            pack[E_AT + 72 * i : E_AT + 72 * i + 72] = wide[which, 3 + i, 72:144]
        pack[E_AT + 216 : E_AT + 252] = wide[which, 7, 36:72]
        pack[S_AT : S_AT + 72] = wide[which, 6, 72:144]
        pack[S_AT + 72 : S_AT + 108] = wide[which, 7, 72:108]
        pack[C_AT : C_AT + 36] = wide[which, 7, 108:144]
        send_out[which] = pack[...].astype(BF)
        halo_out.append(halo_copies(which, send_out, recv_out, out_send, out_recv, ahead))
        for copy in halo_out[-1]:
            copy.start()

    orders = ("xzy", "zyx", "yxz", "xzy")
    going = [None] * 4

    def rdma(b, n, src, dst, peer):
        copy = pltpu.make_async_remote_copy(
            src_ref=src, dst_ref=dst, send_sem=rs_send.at[b, n], recv_sem=rs_recv.at[b, n],
            device_id=peer, device_id_type=MESH,
        )
        copy.start()
        return copy

    def term(b):
        res = tn(xn_s[...], dp_s[:, 512 * b : 512 * b + 512]) if b < 3 else tn(o_s[...], gw[...])
        wg[b] = res.astype(BF).reshape(2, 4, 2, 2, 16, 512)
        going[b] = [rdma(b, 0, wg.at[b, :, :, 1 - core], r0.at[b], partner)]

    def pick(dims, axis, i):
        return tuple(i if dim == axis else slice(None) for dim in dims)

    def stage(b, n):
        for copy in going[b]:
            copy.wait()
        order, dims = orders[b], "zxy"
        held, got = (t0, t1, t2), (r1, r2, r3)
        if n == 0:
            for i in range(2):
                for k in range(4):
                    cut[i, k] = wg[b, i, k, core].astype(F32) + r0[b, i, k].astype(F32)
            for i in range(2):
                for j in range(2):
                    for k in range(4):
                        for m in range(4):
                            t3[2 * i + j, :, k, 4 * m : 4 * m + 4] = cut[i, :, j, 4 * k : 4 * k + 4, 128 * m : 128 * m + 128]
            t0[b] = t3[...].astype(BF)
        else:
            for axis in order[: n - 1]:
                dims = dims.replace(axis, "")
            axis = order[n - 1]
            acc = held[n - 1][(b, *pick(dims, axis, position[axis]))].astype(F32)
            for d in range(3):
                acc = acc + got[n - 1][b, d].astype(F32)
            if n == 3:
                out, first = (qg_ref, 512 * b) if b < 3 else (og_ref, 0)
                for m in range(4):
                    out[:, first + 128 * m : first + 128 * m + 128] = acc[4 * m : 4 * m + 4]
                return
            held[n][b] = acc.astype(BF)
            dims = dims.replace(axis, "")
        axis = order[n]
        going[b] = [
            rdma(b, 3 * n + d, held[n].at[(b, *pick(dims, axis, step(position[axis], d)))], got[n].at[b, d - 1], along[axis][d - 1])
            for d in (1, 2, 3)
        ]

    project(0, 3)
    send(1)
    attend(0, 3)
    halo_arrived(0)
    project(3, 5)
    attend(3, 5)
    finish_out(3, 5)
    send_back(0)
    halo_arrived(1)
    for w in range(NW):
        gw[w * T : w * T + T] = wide[1, w].astype(BF)
    term(3)
    finish_out(0, 3)
    for n in range(2):
        do_s[n] = nn(gw[...], wot_s[:, 256 * n : 256 * n + 256]).astype(BF)
    attend_back(3, 1)
    stage(3, 0)
    attend_back(4, 4)
    finish_grad(3, 5)
    send_back(1)
    stage(3, 1)
    attend_back(0, 3)
    term(0)
    term(1)
    stage(0, 0)
    term(2)
    stage(1, 0)
    stage(3, 2)
    finish_grad(0, 3)
    stage(2, 0)

    def assemble(which, dst):
        for copy in halo_out[which]:
            copy.wait()
        pack[...] = recv_out[which].astype(F32)
        for l in range(2):
            for a in range(24):
                i, ar = (a - 3) // 6, (a - 3) % 6
                at_ = l * 24 + a
                if a < 3:
                    n = l * 3 + a
                    rows_s[at_, 6:18] = pack[S_AT + n * 12 : S_AT + n * 12 + 12]
                    rows_s[at_, 18:24] = pack[S_AT + 72 + n * 6 : S_AT + 72 + n * 6 + 6]
                    rows_s[at_, 0:6] = pack[C_AT + n * 6 : C_AT + n * 6 + 6]
                else:
                    n = l * 6 + ar if i < 3 else l * 3 + ar
                    rows_s[at_, 0:6] = pack[E_AT + 72 * i + n * 6 : E_AT + 72 * i + n * 6 + 6]
                    rows_s[at_, 6:18] = wide[which, window_of(i, 0), n * 12 : n * 12 + 12]
                    rows_s[at_, 18:24] = wide[which, window_of(i, 1), n * 6 : n * 6 + 6]
                dst[l, a] = rows_s[at_].astype(BF)

    assemble(0, of_ref)
    for n in (1, 2):
        for b in range(3):
            stage(b, n)
        if n == 1:
            assemble(1, df_ref)
    for b in range(4):
        stage(b, 3)


def shards(fields, cotangent, qkv_weight, out_weight):
    vm = pl.BlockSpec(memory_space=pltpu.VMEM)
    results = list(
        pl.pallas_call(
            kernel,
            out_shape=[
                pltpu.VMEM((2, 24, 24, D), BF),
                pltpu.VMEM((2, 24, 24, D), BF),
                pltpu.VMEM((4, 3 * D), F32),
                pltpu.VMEM((4, D), F32),
            ],
            in_specs=[pl.BlockSpec(memory_space=pl.ANY)] * 4,
            out_specs=[vm] * 4,
            scratch_shapes=[
                pltpu.VMEM((2, 24, 24, D), BF),
                pltpu.VMEM((2, 24, 24, D), BF),
                pltpu.VMEM((D, 3 * D), BF),
                pltpu.VMEM((D, D), BF),
                pltpu.SemaphoreType.DMA((4,)),
                pltpu.VMEM((2, NW, T, D), F32),
                pltpu.VMEM((48, 24, D), F32),
                pltpu.VMEM((MSG, D), F32),
            ]
            + [pltpu.VMEM((2, MSG, D), BF)] * 4
            + [pltpu.SemaphoreType.DMA((2, 3))] * 4
            + [pltpu.VMEM((TOK, D), BF)] * 3
            + [pltpu.VMEM((2, TOK, 256), BF)] * 4
            + [
                pltpu.VMEM((TOK, D), BF),
                pltpu.VMEM((TOK, 3 * D), BF),
                pltpu.VMEM((NW, 2, T, 8 * T), BF),
                pltpu.VMEM((3 * D, D), BF),
                pltpu.VMEM((D, D), BF),
                pltpu.VMEM((4, 2, 4, 2, 2, 16, 512), BF),
                pltpu.VMEM((4, 2, 4, 2, 16, 512), BF),
                pltpu.VMEM((2, 4, 2, 16, 512), F32),
                pltpu.VMEM((4, 4, 4, 4, 16, 128), BF),
                pltpu.VMEM((4, 3, 4, 4, 16, 128), BF),
                pltpu.VMEM((4, 4, 4, 16, 128), BF),
                pltpu.VMEM((4, 3, 4, 16, 128), BF),
                pltpu.VMEM((4, 4, 16, 128), BF),
                pltpu.VMEM((4, 3, 16, 128), BF),
                pltpu.VMEM((4, 4, 4, 16, 128), F32),
                pltpu.SemaphoreType.DMA((4, 10)),
                pltpu.SemaphoreType.DMA((4, 10)),
            ],
            compiler_params=pltpu.CompilerParams(
                collective_id=0, has_side_effects=True, vmem_limit_bytes=58 * 1024 * 1024
            ),
            cost_estimate=pl.CostEstimate(flops=10 * 10**9, bytes_accessed=8 * 10**6, transcendentals=3 * 10**6),
        )(fields, cotangent, qkv_weight, out_weight)
    )

    def hand_over(*refs):
        copies = [pltpu.make_async_copy(refs[n], refs[4 + n], refs[8].at[n]) for n in range(4)]
        for copy in copies:
            copy.start()
        for copy in copies:
            copy.wait()

    return tuple(
        pl.pallas_call(
            hand_over,
            out_shape=[jax.ShapeDtypeStruct(r.shape, r.dtype) for r in results],
            in_specs=[vm] * 4,
            out_specs=[pl.BlockSpec(memory_space=pl.ANY)] * 4,
            scratch_shapes=[pltpu.SemaphoreType.DMA((4,))],
        )(*[pltpu.with_memory_space_constraint(r, pltpu.VMEM) for r in results])
    )


def solution(mesh):
    placed = (P(None, "lat", "lon", None), P(None, "lat", "lon", None), P(), P())
    return jax.shard_map(
        shards,
        mesh=mesh,
        in_specs=placed,
        out_specs=(
            P(None, "lat", "lon", None),
            P(None, "lat", "lon", None),
            P(("lon", "lat"), None),
            P(("lon", "lat"), None),
        ),
        check_vma=False,
    )
```

```python
import functools, math
import jax
import jax.numpy as jnp
from jax import lax
from jax.experimental import pallas as pl
from jax.experimental.pallas import tpu as pltpu
from jax.sharding import PartitionSpec as P

D = 512
HEADS = 16
HD = 32
T = 144
NW = 8
TOK = NW * T
F32 = jnp.float32
BF = jnp.bfloat16
EPS = 1e-5
SCALE = HD ** -0.5
LOG2E = math.log2(math.e)
LN2 = math.log(2.0)


def nt(a, b):
    return lax.dot_general(a, b, (((1,), (1,)), ((), ())), preferred_element_type=F32)


def nn(a, b):
    return lax.dot_general(a, b, (((1,), (0,)), ((), ())), preferred_element_type=F32)


def tn(a, b):
    return lax.dot_general(a, b, (((0,), (0,)), ((), ())), preferred_element_type=F32)


def norm_stats(x):
    mean = jnp.sum(x, axis=-1, keepdims=True) * (1.0 / D)
    xc = x - mean
    var = jnp.sum(xc * xc, axis=-1, keepdims=True) * (1.0 / D)
    return xc, lax.rsqrt(var + EPS)


def heads_apart(a):
    lane = lax.broadcasted_iota(jnp.int32, (1, 128), 1) // HD
    zero = jnp.zeros((T, 128), BF)
    parts = []
    for h in range(8):
        mask = jnp.where(lane == h % 4, 1.0, 0.0).astype(BF)
        own = a[:, 128 * (h // 4) : 128 * (h // 4) + 128] * mask
        parts.append(jnp.concatenate([own, zero] if h < 4 else [zero, own], axis=1))
    return jnp.concatenate(parts, axis=0)


def heads_together(a):
    lane = lax.broadcasted_iota(jnp.int32, (1, 128), 1) // HD
    halves = []
    for c in range(2):
        cols = slice(128 * c, 128 * c + 128)
        own = a[T * 4 * c : T * 4 * c + T, cols]
        for h in range(1, 4):
            at = T * (4 * c + h)
            own = jnp.where(lane == h, a[at : at + T, cols], own)
        halves.append(own)
    return jnp.concatenate(halves, axis=1)


def attention(w, big, q_s, k_s, v_s, p_s, o_s):
    rows = pl.ds(pl.multiple_of(w * T, 16), T)
    half = T // 2
    query = lax.broadcasted_iota(jnp.int32, (1, 8 * T), 1) % T
    pen0 = jnp.where(query >= half, big, 0.0)
    pen1 = jnp.where(query < half, big, 0.0)
    for g in range(2):
        st = nt(k_s[g, rows, :], heads_apart(q_s[g, rows, :]))
        top = jnp.maximum(
            jnp.max(st[:half], axis=0, keepdims=True) - pen0, jnp.max(st[half:], axis=0, keepdims=True) - pen1
        )
        e = jnp.concatenate([jnp.exp2(st[:half] - (top + pen0)), jnp.exp2(st[half:] - (top + pen1))], axis=0)
        pb = (e * (1.0 / jnp.sum(e, axis=0, keepdims=True))).astype(BF)
        p_s[w, g] = pb
        o_s[rows, 256 * g : 256 * g + 256] = heads_together(tn(pb, v_s[g, rows, :])).astype(BF)


def attention_back(w, q_s, k_s, v_s, p_s, do_s, dp_s):
    rows = pl.ds(pl.multiple_of(w * T, 16), T)
    for g in range(2):
        kg = k_s[g, rows, :]
        qm = heads_apart(q_s[g, rows, :])
        dom = heads_apart(do_s[g, rows, :])
        dpt = nt(v_s[g, rows, :], dom)
        pb = p_s[w, g]
        p = pb.astype(F32)
        ds = (p * (dpt - jnp.sum(p * dpt, axis=0, keepdims=True))).astype(BF)
        dp_s[rows, 1024 + 256 * g : 1280 + 256 * g] = nn(pb, dom).astype(BF)
        dp_s[rows, 512 + 256 * g : 768 + 256 * g] = (nn(ds, qm) * LN2).astype(BF)
        dp_s[rows, 256 * g : 256 * g + 256] = (heads_together(tn(ds, kg)) * SCALE).astype(BF)


MESH = pl.DeviceIdType.MESH
E_AT, S_AT, C_AT, MSG = 0, 256, 368, 416
PARTS = ((E_AT, 256), (S_AT, 112), (C_AT, 48))
FREE = 3 * T


def window_of(i, j):
    if i < 3:
        return i + 3 * j
    return 6 + j


def neighbours(by):
    lon, lat = lax.axis_index("lon"), lax.axis_index("lat")
    nlon, nlat = lax.axis_size("lon"), lax.axis_size("lat")
    lon2, lat2 = lax.rem(lon + by + nlon, nlon), lax.rem(lat + by + nlat, nlat)
    return [(lon2, lat), (lon, lat2), (lon2, lat2)]


def halo_copies(which, send, recv, send_sem, recv_sem, to):
    return [
        pltpu.make_async_remote_copy(
            src_ref=send.at[which, pl.ds(at, rows)],
            dst_ref=recv.at[which, pl.ds(at, rows)],
            send_sem=send_sem.at[which, n],
            recv_sem=recv_sem.at[which, n],
            device_id=peer,
            device_id_type=MESH,
        )
        for n, ((at, rows), peer) in enumerate(zip(PARTS, to))
    ]


def kernel(
    f_any, c_any, w_any, wo_any, of_ref, df_ref, qg_ref, og_ref,
    f_ref, c_ref, w_ref, wo_ref, load_sem,
    wide, rows_s, pack, send_in, recv_in, send_out, recv_out, in_send, in_recv, out_send, out_recv,
    xw, gw, xn_s, q_s, k_s, v_s, do_s, o_s, dp_s, p_s, wt_s, wot_s,
    wg, r0, cut, t0, r1, t1, r2, t3, rs_send, rs_recv,
):
    lon, lat = lax.axis_index("lon"), lax.axis_index("lat")
    core, x, zh = lax.rem(lon, 2), lax.rem(lon // 2, 4), lon // 8
    y, zl = lax.rem(lat, 4), lat // 4
    z = zh * 2 + zl

    def at(zh_, x_, core_, zl_, y_):
        return ((zh_ * 4 + x_) * 2 + core_, zl_ * 4 + y_)

    def step(v, d):
        return lax.rem(v + d, 4)

    partner = at(zh, x, 1 - core, zl, y)
    position = {"x": x, "y": y, "z": z}
    along = {
        "x": [at(zh, step(x, d), core, zl, y) for d in (1, 2, 3)],
        "y": [at(zh, x, core, zl, step(y, d)) for d in (1, 2, 3)],
        "z": [at(step(z, d) // 2, x, core, lax.rem(step(z, d), 2), y) for d in (1, 2, 3)],
    }
    ahead, behind = neighbours(1), neighbours(-1)
    peers = ahead + behind + [partner] + along["x"] + along["y"] + along["z"]
    for m in (1, 2, 3):
        for n in (1, 2, 3):
            zn = step(z, n)
            peers.append(at(zh, step(x, m), core, zl, step(y, n)))
            peers.append(at(zn // 2, step(x, m), core, lax.rem(zn, 2), y))
            peers.append(at(zn // 2, x, core, lax.rem(zn, 2), step(y, m)))
    barrier = pltpu.get_barrier_semaphore()
    for peer in peers:
        pl.semaphore_signal(barrier, inc=1, device_id=peer, device_id_type=MESH)
    loads = [
        pltpu.make_async_copy(src, dst, load_sem.at[n])
        for n, (src, dst) in enumerate(((f_any, f_ref), (c_any, c_ref), (w_any, w_ref), (wo_any, wo_ref)))
    ]
    for load in loads:
        load.start()

    halo_in = []

    def pack_in(which, src):
        loads[which].wait()
        for l in range(2):
            for a in range(24):
                i, ar = (a - 3) // 6, (a - 3) % 6
                if a < 3:
                    row = src[l, a].astype(F32)
                    n = l * 3 + a
                    pack[S_AT + n * 12 : S_AT + n * 12 + 12] = row[6:18]
                    pack[S_AT + 72 + n * 6 : S_AT + 72 + n * 6 + 6] = row[18:24]
                    pack[C_AT + n * 6 : C_AT + n * 6 + 6] = row[0:6]
                else:
                    row = src[l, a, 0:16].astype(F32)
                    n = l * 6 + ar if i < 3 else l * 3 + ar
                    pack[E_AT + 72 * i + n * 6 : E_AT + 72 * i + n * 6 + 6] = row[0:6]
        send_in[which] = pack[...].astype(BF)

    def send(which):
        halo_in.append(halo_copies(which, send_in, recv_in, in_send, in_recv, behind))
        for copy in halo_in[-1]:
            copy.start()

    def own(which, src):
        for l in range(2):
            for a in range(3, 24):
                i, ar = (a - 3) // 6, (a - 3) % 6
                row = src[l, a].astype(F32)
                n = l * 6 + ar if i < 3 else l * 3 + ar
                wide[which, window_of(i, 0), n * 12 : n * 12 + 12] = row[6:18]
                wide[which, window_of(i, 1), n * 6 : n * 6 + 6] = row[18:24]

    pack_in(0, f_ref)
    own(0, f_ref)
    pl.semaphore_wait(barrier, len(peers))
    send(0)
    pack_in(1, c_ref)
    own(1, c_ref)
    loads[2].wait()
    loads[3].wait()
    wt_s[...] = w_ref[...].T
    wot_s[...] = wo_ref[...].T

    def project(first, count):
        rows = slice(first * T, (first + count) * T)
        for w in range(first, first + count):
            at_ = slice(w * T, w * T + T)
            xv = wide[0, w]
            xw[at_] = xv.astype(BF)
            xc, rstd = norm_stats(xv)
            xn_s[at_] = (xc * rstd).astype(BF)
        for part, (dst, scale) in enumerate(((q_s, SCALE * LOG2E), (k_s, None), (v_s, None))):
            for n in range(2):
                res = nn(xn_s[rows], w_ref[:, 512 * part + 256 * n : 512 * part + 256 * n + 256])
                if scale is not None:
                    res = res * scale
                dst[n, rows] = res.astype(BF)

    last = jnp.where(lat == lax.axis_size("lat") - 1, 1e9, 0.0)

    def attend(first, count):
        def window(w, _):
            big = jnp.where(w >= NW - 2, last, 0.0).astype(F32)
            attention(w, big, q_s, k_s, v_s, p_s, o_s)
            return 0

        lax.fori_loop(first, first + count, window, 0)

    def project_grad(first, count):
        rows = slice(first * T, (first + count) * T)
        for w in range(first, first + count):
            gw[w * T : w * T + T] = wide[1, w].astype(BF)
        for n in range(2):
            do_s[n, rows] = nn(gw[rows], wot_s[:, 256 * n : 256 * n + 256]).astype(BF)

    def attend_back(first, count):
        def window(w, _):
            attention_back(w, q_s, k_s, v_s, p_s, do_s, dp_s)
            return 0

        lax.fori_loop(first, first + count, window, 0)

    def finish_out(first, count):
        for w in range(first, first + count):
            at_ = slice(w * T, w * T + T)
            wide[0, w] = xw[at_].astype(F32) + nn(o_s[at_], wo_ref[...])

    def finish_grad(first, count):
        for w in range(first, first + count):
            at_ = slice(w * T, w * T + T)
            gn = nn(dp_s[at_], wt_s[...])
            xc, rstd = norm_stats(xw[at_].astype(F32))
            xh = xc * rstd
            m1 = jnp.sum(gn, axis=-1, keepdims=True) * (1.0 / D)
            m2 = jnp.sum(gn * xh, axis=-1, keepdims=True) * (1.0 / D)
            wide[1, w] = gw[at_].astype(F32) + rstd * (gn - m1 - xh * m2)

    def halo_arrived(which):
        for copy in halo_in[which]:
            copy.wait()
        pack[...] = recv_in[which].astype(F32)
        for i in range(3):
            wide[which, 3 + i, 72:144] = pack[E_AT + 72 * i : E_AT + 72 * i + 72]
        wide[which, 7, 36:72] = pack[E_AT + 216 : E_AT + 252]
        wide[which, 6, 72:144] = pack[S_AT : S_AT + 72]
        wide[which, 7, 72:108] = pack[S_AT + 72 : S_AT + 108]
        wide[which, 7, 108:144] = pack[C_AT : C_AT + 36]

    halo_out = []

    def send_back(which):
        for i in range(3):
            pack[E_AT + 72 * i : E_AT + 72 * i + 72] = wide[which, 3 + i, 72:144]
        pack[E_AT + 216 : E_AT + 252] = wide[which, 7, 36:72]
        pack[S_AT : S_AT + 72] = wide[which, 6, 72:144]
        pack[S_AT + 72 : S_AT + 108] = wide[which, 7, 72:108]
        pack[C_AT : C_AT + 36] = wide[which, 7, 108:144]
        send_out[which] = pack[...].astype(BF)
        halo_out.append(halo_copies(which, send_out, recv_out, out_send, out_recv, ahead))
        for copy in halo_out[-1]:
            copy.start()

    axes = ("x", "z", "y", "x")
    going = [None] * 4

    def rdma(b, n, src, dst, peer):
        copy = pltpu.make_async_remote_copy(
            src_ref=src, dst_ref=dst, send_sem=rs_send.at[b, n], recv_sem=rs_recv.at[b, n],
            device_id=peer, device_id_type=MESH,
        )
        copy.start()
        return copy

    def term(b):
        res = tn(xn_s[...], dp_s[:, 512 * b : 512 * b + 512]) if b < 3 else tn(o_s[...], gw[...])
        wg[b] = res.astype(BF).reshape(2, 4, 2, 2, 16, 512)
        going[b] = [rdma(b, 0, wg.at[b, :, :, 1 - core], r0.at[b], partner)]

    def pick(dims, axis, i):
        return tuple(i if dim == axis else slice(None) for dim in dims)

    def device(spot):
        return at(spot["z"] // 2, spot["x"], core, lax.rem(spot["z"], 2), spot["y"])

    def stage(b, n):
        for copy in going[b]:
            copy.wait()
        axis = axes[b]
        p, q = "zxy".replace(axis, "")
        if n == 0:
            for i in range(2):
                for k in range(4):
                    cut[i, k] = wg[b, i, k, core].astype(F32) + r0[b, i, k].astype(F32)
            for i in range(2):
                for j in range(2):
                    for k in range(4):
                        for m in range(4):
                            t3[2 * i + j, :, k, 4 * m : 4 * m + 4] = cut[i, :, j, 4 * k : 4 * k + 4, 128 * m : 128 * m + 128]
            t0[b] = t3[...].astype(BF)
            going[b] = [
                rdma(b, d, t0.at[(b, *pick("zxy", axis, step(position[axis], d)))], r1.at[b, d - 1], along[axis][d - 1])
                for d in (1, 2, 3)
            ]
        elif n == 1:
            acc = t0[(b, *pick("zxy", axis, position[axis]))].astype(F32)
            for d in range(3):
                acc = acc + r1[b, d].astype(F32)
            t1[b] = acc.astype(BF)
            going[b] = []
            for m in range(15, 0, -1):
                spot = dict(position)
                spot[p], spot[q] = step(position[p], m // 4), step(position[q], m % 4)
                going[b].append(rdma(b, 3 + m, t1.at[b, spot[p], spot[q]], r2.at[b, m - 1], device(spot)))
        else:
            acc = t1[b, position[p], position[q]].astype(F32)
            for m in range(15):
                acc = acc + r2[b, m].astype(F32)
            out, first = (qg_ref, 512 * b) if b < 3 else (og_ref, 0)
            for m in range(4):
                out[:, first + 128 * m : first + 128 * m + 128] = acc[4 * m : 4 * m + 4]

    project(0, 3)
    send(1)
    project_grad(0, 3)
    attend(0, 3)
    attend_back(0, 3)

    halo_arrived(0)
    project(3, 5)
    attend(3, 5)
    halo_arrived(1)
    project_grad(3, 5)
    term(3)
    finish_out(3, 5)
    send_back(0)
    attend_back(3, 2)
    stage(3, 0)
    attend_back(5, 3)
    finish_grad(3, 5)
    send_back(1)

    term(0)
    term(1)
    stage(0, 0)
    term(2)
    stage(1, 0)
    stage(2, 0)
    stage(3, 1)
    finish_grad(0, 3)
    finish_out(0, 3)

    def assemble(which, dst):
        for copy in halo_out[which]:
            copy.wait()
        pack[...] = recv_out[which].astype(F32)
        for l in range(2):
            for a in range(24):
                i, ar = (a - 3) // 6, (a - 3) % 6
                at_ = l * 24 + a
                if a < 3:
                    n = l * 3 + a
                    rows_s[at_, 6:18] = pack[S_AT + n * 12 : S_AT + n * 12 + 12]
                    rows_s[at_, 18:24] = pack[S_AT + 72 + n * 6 : S_AT + 72 + n * 6 + 6]
                    rows_s[at_, 0:6] = pack[C_AT + n * 6 : C_AT + n * 6 + 6]
                else:
                    n = l * 6 + ar if i < 3 else l * 3 + ar
                    rows_s[at_, 0:6] = pack[E_AT + 72 * i + n * 6 : E_AT + 72 * i + n * 6 + 6]
                    rows_s[at_, 6:18] = wide[which, window_of(i, 0), n * 12 : n * 12 + 12]
                    rows_s[at_, 18:24] = wide[which, window_of(i, 1), n * 6 : n * 6 + 6]
                dst[l, a] = rows_s[at_].astype(BF)

    assemble(0, of_ref)
    for b in range(3):
        stage(b, 1)
    stage(3, 2)
    assemble(1, df_ref)
    for b in range(3):
        stage(b, 2)


def shards(fields, cotangent, qkv_weight, out_weight):
    vm = pl.BlockSpec(memory_space=pltpu.VMEM)
    results = list(
        pl.pallas_call(
            kernel,
            out_shape=[
                pltpu.VMEM((2, 24, 24, D), BF),
                pltpu.VMEM((2, 24, 24, D), BF),
                pltpu.VMEM((4, 3 * D), F32),
                pltpu.VMEM((4, D), F32),
            ],
            in_specs=[pl.BlockSpec(memory_space=pl.ANY)] * 4,
            out_specs=[vm] * 4,
            scratch_shapes=[
                pltpu.VMEM((2, 24, 24, D), BF),
                pltpu.VMEM((2, 24, 24, D), BF),
                pltpu.VMEM((D, 3 * D), BF),
                pltpu.VMEM((D, D), BF),
                pltpu.SemaphoreType.DMA((4,)),
                pltpu.VMEM((2, NW, T, D), F32),
                pltpu.VMEM((48, 24, D), F32),
                pltpu.VMEM((MSG, D), F32),
            ]
            + [pltpu.VMEM((2, MSG, D), BF)] * 4
            + [pltpu.SemaphoreType.DMA((2, 3))] * 4
            + [pltpu.VMEM((TOK, D), BF)] * 3
            + [pltpu.VMEM((2, TOK, 256), BF)] * 4
            + [
                pltpu.VMEM((TOK, D), BF),
                pltpu.VMEM((TOK, 3 * D), BF),
                pltpu.VMEM((NW, 2, T, 8 * T), BF),
                pltpu.VMEM((3 * D, D), BF),
                pltpu.VMEM((D, D), BF),
                pltpu.VMEM((4, 2, 4, 2, 2, 16, 512), BF),
                pltpu.VMEM((4, 2, 4, 2, 16, 512), BF),
                pltpu.VMEM((2, 4, 2, 16, 512), F32),
                pltpu.VMEM((4, 4, 4, 4, 16, 128), BF),
                pltpu.VMEM((4, 3, 4, 4, 16, 128), BF),
                pltpu.VMEM((4, 4, 4, 16, 128), BF),
                pltpu.VMEM((4, 15, 16, 128), BF),
                pltpu.VMEM((4, 4, 4, 16, 128), F32),
                pltpu.SemaphoreType.DMA((4, 19)),
                pltpu.SemaphoreType.DMA((4, 19)),
            ],
            compiler_params=pltpu.CompilerParams(
                collective_id=0, has_side_effects=True, vmem_limit_bytes=58 * 1024 * 1024
            ),
            cost_estimate=pl.CostEstimate(flops=10 * 10**9, bytes_accessed=8 * 10**6, transcendentals=3 * 10**6),
        )(fields, cotangent, qkv_weight, out_weight)
    )

    def hand_over(*refs):
        copies = [pltpu.make_async_copy(refs[n], refs[4 + n], refs[8].at[n]) for n in range(4)]
        for copy in copies:
            copy.start()
        for copy in copies:
            copy.wait()

    return tuple(
        pl.pallas_call(
            hand_over,
            out_shape=[jax.ShapeDtypeStruct(r.shape, r.dtype) for r in results],
            in_specs=[vm] * 4,
            out_specs=[pl.BlockSpec(memory_space=pl.ANY)] * 4,
            scratch_shapes=[pltpu.SemaphoreType.DMA((4,))],
        )(*[pltpu.with_memory_space_constraint(r, pltpu.VMEM) for r in results])
    )


def solution(mesh):
    placed = (P(None, "lat", "lon", None), P(None, "lat", "lon", None), P(), P())
    return jax.shard_map(
        shards,
        mesh=mesh,
        in_specs=placed,
        out_specs=(
            P(None, "lat", "lon", None),
            P(None, "lat", "lon", None),
            P(("lon", "lat"), None),
            P(("lon", "lat"), None),
        ),
        check_vma=False,
    )
```

```python
import functools, math
import jax
import jax.numpy as jnp
from jax import lax
from jax.experimental import pallas as pl
from jax.experimental.pallas import tpu as pltpu
from jax.sharding import PartitionSpec as P

D = 512
HEADS = 16
HD = 32
T = 144
NW = 8
TOK = NW * T
F32 = jnp.float32
BF = jnp.bfloat16
EPS = 1e-5
SCALE = HD ** -0.5
LOG2E = math.log2(math.e)
LN2 = math.log(2.0)


def nt(a, b):
    return lax.dot_general(a, b, (((1,), (1,)), ((), ())), preferred_element_type=F32)


def nn(a, b):
    return lax.dot_general(a, b, (((1,), (0,)), ((), ())), preferred_element_type=F32)


def tn(a, b):
    return lax.dot_general(a, b, (((0,), (0,)), ((), ())), preferred_element_type=F32)


def norm_stats(x):
    mean = jnp.sum(x, axis=-1, keepdims=True) * (1.0 / D)
    xc = x - mean
    var = jnp.sum(xc * xc, axis=-1, keepdims=True) * (1.0 / D)
    return xc, lax.rsqrt(var + EPS)


def heads_apart(a):
    lane = lax.broadcasted_iota(jnp.int32, (1, 128), 1) // HD
    zero = jnp.zeros((T, 128), BF)
    parts = []
    for h in range(8):
        mask = jnp.where(lane == h % 4, 1.0, 0.0).astype(BF)
        own = a[:, 128 * (h // 4) : 128 * (h // 4) + 128] * mask
        parts.append(jnp.concatenate([own, zero] if h < 4 else [zero, own], axis=1))
    return jnp.concatenate(parts, axis=0)


def heads_together(a):
    lane = lax.broadcasted_iota(jnp.int32, (1, 128), 1) // HD
    halves = []
    for c in range(2):
        cols = slice(128 * c, 128 * c + 128)
        own = a[T * 4 * c : T * 4 * c + T, cols]
        for h in range(1, 4):
            at = T * (4 * c + h)
            own = jnp.where(lane == h, a[at : at + T, cols], own)
        halves.append(own)
    return jnp.concatenate(halves, axis=1)


def attention(w, big, q_s, k_s, v_s, p_s, o_s):
    rows = slice(w * T, w * T + T)
    half = T // 2
    if big is not None:
        query = lax.broadcasted_iota(jnp.int32, (1, 8 * T), 1) % T
        pen0 = jnp.where(query >= half, big, 0.0)
        pen1 = jnp.where(query < half, big, 0.0)
    for g in range(2):
        st = nt(k_s[g, rows, :], heads_apart(q_s[g, rows, :]))
        if big is None:
            e = jnp.exp2(st - jnp.max(st, axis=0, keepdims=True))
        else:
            top = jnp.maximum(
                jnp.max(st[:half], axis=0, keepdims=True) - pen0, jnp.max(st[half:], axis=0, keepdims=True) - pen1
            )
            e = jnp.concatenate([jnp.exp2(st[:half] - (top + pen0)), jnp.exp2(st[half:] - (top + pen1))], axis=0)
        pb = (e * (1.0 / jnp.sum(e, axis=0, keepdims=True))).astype(BF)
        p_s[w, g] = pb
        o_s[rows, 256 * g : 256 * g + 256] = heads_together(tn(pb, v_s[g, rows, :])).astype(BF)


def attention_back(w, q_s, k_s, v_s, p_s, do_s, dp_s):
    rows = slice(w * T, w * T + T)
    for g in range(2):
        kg = k_s[g, rows, :]
        qm = heads_apart(q_s[g, rows, :])
        dom = heads_apart(do_s[g, rows, :])
        dpt = nt(v_s[g, rows, :], dom)
        pb = p_s[w, g]
        p = pb.astype(F32)
        ds = (p * (dpt - jnp.sum(p * dpt, axis=0, keepdims=True))).astype(BF)
        dp_s[rows, 1024 + 256 * g : 1280 + 256 * g] = nn(pb, dom).astype(BF)
        dp_s[rows, 512 + 256 * g : 768 + 256 * g] = (nn(ds, qm) * LN2).astype(BF)
        dp_s[rows, 256 * g : 256 * g + 256] = (heads_together(tn(ds, kg)) * SCALE).astype(BF)


MESH = pl.DeviceIdType.MESH
E_AT, S_AT, C_AT, MSG = 0, 256, 368, 416
PARTS = ((E_AT, 256), (S_AT, 112), (C_AT, 48))
FREE = 3 * T


def window_of(i, j):
    if i < 3:
        return i + 3 * j
    return 6 + j


def neighbours(by):
    lon, lat = lax.axis_index("lon"), lax.axis_index("lat")
    nlon, nlat = lax.axis_size("lon"), lax.axis_size("lat")
    lon2, lat2 = lax.rem(lon + by + nlon, nlon), lax.rem(lat + by + nlat, nlat)
    return [(lon2, lat), (lon, lat2), (lon2, lat2)]


def halo_copies(which, send, recv, send_sem, recv_sem, to):
    return [
        pltpu.make_async_remote_copy(
            src_ref=send.at[which, pl.ds(at, rows)],
            dst_ref=recv.at[which, pl.ds(at, rows)],
            send_sem=send_sem.at[which, n],
            recv_sem=recv_sem.at[which, n],
            device_id=peer,
            device_id_type=MESH,
        )
        for n, ((at, rows), peer) in enumerate(zip(PARTS, to))
    ]


def kernel(
    f_any, c_any, w_any, wo_any, of_ref, df_ref, qg_ref, og_ref,
    f_ref, c_ref, w_ref, wo_ref, load_sem,
    wide, rows_s, pack, send_in, recv_in, send_out, recv_out, in_send, in_recv, out_send, out_recv,
    xw, gw, xn_s, q_s, k_s, v_s, do_s, o_s, dp_s, p_s, wt_s, wot_s,
    wg, r0, cut, t0, r1, t1, r2, t3, rs_send, rs_recv,
):
    lon, lat = lax.axis_index("lon"), lax.axis_index("lat")
    core, x, zh = lax.rem(lon, 2), lax.rem(lon // 2, 4), lon // 8
    y, zl = lax.rem(lat, 4), lat // 4
    z = zh * 2 + zl

    def at(zh_, x_, core_, zl_, y_):
        return ((zh_ * 4 + x_) * 2 + core_, zl_ * 4 + y_)

    def step(v, d):
        return lax.rem(v + d, 4)

    partner = at(zh, x, 1 - core, zl, y)
    position = {"x": x, "y": y, "z": z}
    along = {
        "x": [at(zh, step(x, d), core, zl, y) for d in (1, 2, 3)],
        "y": [at(zh, x, core, zl, step(y, d)) for d in (1, 2, 3)],
        "z": [at(step(z, d) // 2, x, core, lax.rem(step(z, d), 2), y) for d in (1, 2, 3)],
    }
    ahead, behind = neighbours(1), neighbours(-1)
    peers = ahead + behind + [partner] + along["x"] + along["y"] + along["z"]
    for m in (1, 2, 3):
        for n in (1, 2, 3):
            zn = step(z, n)
            peers.append(at(zh, step(x, m), core, zl, step(y, n)))
            peers.append(at(zn // 2, step(x, m), core, lax.rem(zn, 2), y))
            peers.append(at(zn // 2, x, core, lax.rem(zn, 2), step(y, m)))
    barrier = pltpu.get_barrier_semaphore()
    for peer in peers:
        pl.semaphore_signal(barrier, inc=1, device_id=peer, device_id_type=MESH)
    loads = [
        pltpu.make_async_copy(src, dst, load_sem.at[n])
        for n, (src, dst) in enumerate(((f_any, f_ref), (c_any, c_ref), (w_any, w_ref), (wo_any, wo_ref)))
    ]
    for load in loads:
        load.start()

    halo_in = []

    def pack_in(which, src):
        loads[which].wait()
        for l in range(2):
            for a in range(24):
                i, ar = (a - 3) // 6, (a - 3) % 6
                if a < 3:
                    row = src[l, a].astype(F32)
                    n = l * 3 + a
                    pack[S_AT + n * 12 : S_AT + n * 12 + 12] = row[6:18]
                    pack[S_AT + 72 + n * 6 : S_AT + 72 + n * 6 + 6] = row[18:24]
                    pack[C_AT + n * 6 : C_AT + n * 6 + 6] = row[0:6]
                else:
                    row = src[l, a, 0:16].astype(F32)
                    n = l * 6 + ar if i < 3 else l * 3 + ar
                    pack[E_AT + 72 * i + n * 6 : E_AT + 72 * i + n * 6 + 6] = row[0:6]
        send_in[which] = pack[...].astype(BF)

    def send(which):
        halo_in.append(halo_copies(which, send_in, recv_in, in_send, in_recv, behind))
        for copy in halo_in[-1]:
            copy.start()

    def own(which, src):
        for l in range(2):
            for a in range(3, 24):
                i, ar = (a - 3) // 6, (a - 3) % 6
                row = src[l, a].astype(F32)
                n = l * 6 + ar if i < 3 else l * 3 + ar
                wide[which, window_of(i, 0), n * 12 : n * 12 + 12] = row[6:18]
                wide[which, window_of(i, 1), n * 6 : n * 6 + 6] = row[18:24]

    pack_in(0, f_ref)
    own(0, f_ref)
    pl.semaphore_wait(barrier, len(peers))
    send(0)
    pack_in(1, c_ref)
    own(1, c_ref)
    loads[2].wait()
    loads[3].wait()
    wt_s[...] = w_ref[...].T
    wot_s[...] = wo_ref[...].T

    def project(first, count):
        rows = slice(first * T, (first + count) * T)
        for w in range(first, first + count):
            at_ = slice(w * T, w * T + T)
            xv = wide[0, w]
            xw[at_] = xv.astype(BF)
            xc, rstd = norm_stats(xv)
            xn_s[at_] = (xc * rstd).astype(BF)
        for part, (dst, scale) in enumerate(((q_s, SCALE * LOG2E), (k_s, None), (v_s, None))):
            for n in range(2):
                res = nn(xn_s[rows], w_ref[:, 512 * part + 256 * n : 512 * part + 256 * n + 256])
                if scale is not None:
                    res = res * scale
                dst[n, rows] = res.astype(BF)

    last = jnp.where(lat == lax.axis_size("lat") - 1, 1e9, 0.0)

    def attend(first, count):
        for w in range(first, first + count):
            attention(w, last if w >= NW - 2 else None, q_s, k_s, v_s, p_s, o_s)

    def project_grad(first, count):
        rows = slice(first * T, (first + count) * T)
        for w in range(first, first + count):
            gw[w * T : w * T + T] = wide[1, w].astype(BF)
        for n in range(2):
            do_s[n, rows] = nn(gw[rows], wot_s[:, 256 * n : 256 * n + 256]).astype(BF)

    def attend_back(first, count):
        for w in range(first, first + count):
            attention_back(w, q_s, k_s, v_s, p_s, do_s, dp_s)

    def finish_out(first, count):
        for w in range(first, first + count):
            at_ = slice(w * T, w * T + T)
            wide[0, w] = xw[at_].astype(F32) + nn(o_s[at_], wo_ref[...])

    def finish_grad(first, count):
        for w in range(first, first + count):
            at_ = slice(w * T, w * T + T)
            gn = nn(dp_s[at_], wt_s[...])
            xc, rstd = norm_stats(xw[at_].astype(F32))
            xh = xc * rstd
            m1 = jnp.sum(gn, axis=-1, keepdims=True) * (1.0 / D)
            m2 = jnp.sum(gn * xh, axis=-1, keepdims=True) * (1.0 / D)
            wide[1, w] = gw[at_].astype(F32) + rstd * (gn - m1 - xh * m2)

    def halo_arrived(which):
        for copy in halo_in[which]:
            copy.wait()
        pack[...] = recv_in[which].astype(F32)
        for i in range(3):
            wide[which, 3 + i, 72:144] = pack[E_AT + 72 * i : E_AT + 72 * i + 72]
        wide[which, 7, 36:72] = pack[E_AT + 216 : E_AT + 252]
        wide[which, 6, 72:144] = pack[S_AT : S_AT + 72]
        wide[which, 7, 72:108] = pack[S_AT + 72 : S_AT + 108]
        wide[which, 7, 108:144] = pack[C_AT : C_AT + 36]

    halo_out = []

    def send_back(which):
        for i in range(3):
            pack[E_AT + 72 * i : E_AT + 72 * i + 72] = wide[which, 3 + i, 72:144]
        pack[E_AT + 216 : E_AT + 252] = wide[which, 7, 36:72]
        pack[S_AT : S_AT + 72] = wide[which, 6, 72:144]
        pack[S_AT + 72 : S_AT + 108] = wide[which, 7, 72:108]
        pack[C_AT : C_AT + 36] = wide[which, 7, 108:144]
        send_out[which] = pack[...].astype(BF)
        halo_out.append(halo_copies(which, send_out, recv_out, out_send, out_recv, ahead))
        for copy in halo_out[-1]:
            copy.start()

    axes = ("x", "z", "y", "x")
    going = [None] * 4

    def rdma(b, n, src, dst, peer):
        copy = pltpu.make_async_remote_copy(
            src_ref=src, dst_ref=dst, send_sem=rs_send.at[b, n], recv_sem=rs_recv.at[b, n],
            device_id=peer, device_id_type=MESH,
        )
        copy.start()
        return copy

    def term(b):
        res = tn(xn_s[...], dp_s[:, 512 * b : 512 * b + 512]) if b < 3 else tn(o_s[...], gw[...])
        wg[b] = res.astype(BF).reshape(2, 4, 2, 2, 16, 512)
        going[b] = [rdma(b, 0, wg.at[b, :, :, 1 - core], r0.at[b], partner)]

    def pick(dims, axis, i):
        return tuple(i if dim == axis else slice(None) for dim in dims)

    def device(spot):
        return at(spot["z"] // 2, spot["x"], core, lax.rem(spot["z"], 2), spot["y"])

    def stage(b, n):
        for copy in going[b]:
            copy.wait()
        axis = axes[b]
        p, q = "zxy".replace(axis, "")
        if n == 0:
            for i in range(2):
                for k in range(4):
                    cut[i, k] = wg[b, i, k, core].astype(F32) + r0[b, i, k].astype(F32)
            for i in range(2):
                for j in range(2):
                    for k in range(4):
                        for m in range(4):
                            t3[2 * i + j, :, k, 4 * m : 4 * m + 4] = cut[i, :, j, 4 * k : 4 * k + 4, 128 * m : 128 * m + 128]
            t0[b] = t3[...].astype(BF)
            going[b] = [
                rdma(b, d, t0.at[(b, *pick("zxy", axis, step(position[axis], d)))], r1.at[b, d - 1], along[axis][d - 1])
                for d in (1, 2, 3)
            ]
        elif n == 1:
            acc = t0[(b, *pick("zxy", axis, position[axis]))].astype(F32)
            for d in range(3):
                acc = acc + r1[b, d].astype(F32)
            t1[b] = acc.astype(BF)
            going[b] = []
            for m in range(15, 0, -1):
                spot = dict(position)
                spot[p], spot[q] = step(position[p], m // 4), step(position[q], m % 4)
                going[b].append(rdma(b, 3 + m, t1.at[b, spot[p], spot[q]], r2.at[b, m - 1], device(spot)))
        else:
            acc = t1[b, position[p], position[q]].astype(F32)
            for m in range(15):
                acc = acc + r2[b, m].astype(F32)
            out, first = (qg_ref, 512 * b) if b < 3 else (og_ref, 0)
            for m in range(4):
                out[:, first + 128 * m : first + 128 * m + 128] = acc[4 * m : 4 * m + 4]

    project(0, 3)
    send(1)
    project_grad(0, 3)
    attend(0, 3)
    attend_back(0, 3)

    halo_arrived(0)
    project(3, 5)
    attend(3, 5)
    halo_arrived(1)
    project_grad(3, 5)
    term(3)
    finish_out(3, 5)
    send_back(0)
    stage(3, 0)
    attend_back(3, 5)
    finish_grad(3, 5)
    send_back(1)

    term(0)
    term(1)
    stage(0, 0)
    term(2)
    stage(1, 0)
    stage(2, 0)
    stage(3, 1)
    finish_grad(0, 3)
    finish_out(0, 3)

    def assemble(which, dst):
        for copy in halo_out[which]:
            copy.wait()
        pack[...] = recv_out[which].astype(F32)
        for l in range(2):
            for a in range(24):
                i, ar = (a - 3) // 6, (a - 3) % 6
                at_ = l * 24 + a
                if a < 3:
                    n = l * 3 + a
                    rows_s[at_, 6:18] = pack[S_AT + n * 12 : S_AT + n * 12 + 12]
                    rows_s[at_, 18:24] = pack[S_AT + 72 + n * 6 : S_AT + 72 + n * 6 + 6]
                    rows_s[at_, 0:6] = pack[C_AT + n * 6 : C_AT + n * 6 + 6]
                else:
                    n = l * 6 + ar if i < 3 else l * 3 + ar
                    rows_s[at_, 0:6] = pack[E_AT + 72 * i + n * 6 : E_AT + 72 * i + n * 6 + 6]
                    rows_s[at_, 6:18] = wide[which, window_of(i, 0), n * 12 : n * 12 + 12]
                    rows_s[at_, 18:24] = wide[which, window_of(i, 1), n * 6 : n * 6 + 6]
                dst[l, a] = rows_s[at_].astype(BF)

    assemble(0, of_ref)
    for b in range(3):
        stage(b, 1)
    stage(3, 2)
    assemble(1, df_ref)
    for b in range(3):
        stage(b, 2)


def shards(fields, cotangent, qkv_weight, out_weight):
    vm = pl.BlockSpec(memory_space=pltpu.VMEM)
    results = list(
        pl.pallas_call(
            kernel,
            out_shape=[
                pltpu.VMEM((2, 24, 24, D), BF),
                pltpu.VMEM((2, 24, 24, D), BF),
                pltpu.VMEM((4, 3 * D), F32),
                pltpu.VMEM((4, D), F32),
            ],
            in_specs=[pl.BlockSpec(memory_space=pl.ANY)] * 4,
            out_specs=[vm] * 4,
            scratch_shapes=[
                pltpu.VMEM((2, 24, 24, D), BF),
                pltpu.VMEM((2, 24, 24, D), BF),
                pltpu.VMEM((D, 3 * D), BF),
                pltpu.VMEM((D, D), BF),
                pltpu.SemaphoreType.DMA((4,)),
                pltpu.VMEM((2, NW, T, D), F32),
                pltpu.VMEM((48, 24, D), F32),
                pltpu.VMEM((MSG, D), F32),
            ]
            + [pltpu.VMEM((2, MSG, D), BF)] * 4
            + [pltpu.SemaphoreType.DMA((2, 3))] * 4
            + [pltpu.VMEM((TOK, D), BF)] * 3
            + [pltpu.VMEM((2, TOK, 256), BF)] * 4
            + [
                pltpu.VMEM((TOK, D), BF),
                pltpu.VMEM((TOK, 3 * D), BF),
                pltpu.VMEM((NW, 2, T, 8 * T), BF),
                pltpu.VMEM((3 * D, D), BF),
                pltpu.VMEM((D, D), BF),
                pltpu.VMEM((4, 2, 4, 2, 2, 16, 512), BF),
                pltpu.VMEM((4, 2, 4, 2, 16, 512), BF),
                pltpu.VMEM((2, 4, 2, 16, 512), F32),
                pltpu.VMEM((4, 4, 4, 4, 16, 128), BF),
                pltpu.VMEM((4, 3, 4, 4, 16, 128), BF),
                pltpu.VMEM((4, 4, 4, 16, 128), BF),
                pltpu.VMEM((4, 15, 16, 128), BF),
                pltpu.VMEM((4, 4, 4, 16, 128), F32),
                pltpu.SemaphoreType.DMA((4, 19)),
                pltpu.SemaphoreType.DMA((4, 19)),
            ],
            compiler_params=pltpu.CompilerParams(
                collective_id=0, has_side_effects=True, vmem_limit_bytes=58 * 1024 * 1024
            ),
            cost_estimate=pl.CostEstimate(flops=10 * 10**9, bytes_accessed=8 * 10**6, transcendentals=3 * 10**6),
        )(fields, cotangent, qkv_weight, out_weight)
    )

    def hand_over(*refs):
        copies = [pltpu.make_async_copy(refs[n], refs[4 + n], refs[8].at[n]) for n in range(4)]
        for copy in copies:
            copy.start()
        for copy in copies:
            copy.wait()

    return tuple(
        pl.pallas_call(
            hand_over,
            out_shape=[jax.ShapeDtypeStruct(r.shape, r.dtype) for r in results],
            in_specs=[vm] * 4,
            out_specs=[pl.BlockSpec(memory_space=pl.ANY)] * 4,
            scratch_shapes=[pltpu.SemaphoreType.DMA((4,))],
        )(*[pltpu.with_memory_space_constraint(r, pltpu.VMEM) for r in results])
    )


def solution(mesh):
    placed = (P(None, "lat", "lon", None), P(None, "lat", "lon", None), P(), P())
    return jax.shard_map(
        shards,
        mesh=mesh,
        in_specs=placed,
        out_specs=(
            P(None, "lat", "lon", None),
            P(None, "lat", "lon", None),
            P(("lon", "lat"), None),
            P(("lon", "lat"), None),
        ),
        check_vma=False,
    )
```

```python
import functools, math
import jax
import jax.numpy as jnp
from jax import lax
from jax.experimental import pallas as pl
from jax.experimental.pallas import tpu as pltpu
from jax.sharding import PartitionSpec as P

D = 512
HEADS = 16
HD = 32
T = 144
NW = 8
TOK = NW * T
F32 = jnp.float32
BF = jnp.bfloat16
EPS = 1e-5
SCALE = HD ** -0.5
LOG2E = math.log2(math.e)
LN2 = math.log(2.0)


def nt(a, b):
    return lax.dot_general(a, b, (((1,), (1,)), ((), ())), preferred_element_type=F32)


def nn(a, b):
    return lax.dot_general(a, b, (((1,), (0,)), ((), ())), preferred_element_type=F32)


def tn(a, b):
    return lax.dot_general(a, b, (((0,), (0,)), ((), ())), preferred_element_type=F32)


def norm_stats(x):
    mean = jnp.sum(x, axis=-1, keepdims=True) * (1.0 / D)
    xc = x - mean
    var = jnp.sum(xc * xc, axis=-1, keepdims=True) * (1.0 / D)
    return xc, lax.rsqrt(var + EPS)


def heads_apart(a):
    lane = lax.broadcasted_iota(jnp.int32, (1, 128), 1) // HD
    zero = jnp.zeros((T, 128), BF)
    parts = []
    for h in range(8):
        mask = jnp.where(lane == h % 4, 1.0, 0.0).astype(BF)
        own = a[:, 128 * (h // 4) : 128 * (h // 4) + 128] * mask
        parts.append(jnp.concatenate([own, zero] if h < 4 else [zero, own], axis=1))
    return jnp.concatenate(parts, axis=0)


def heads_together(a):
    lane = lax.broadcasted_iota(jnp.int32, (1, 128), 1) // HD
    halves = []
    for c in range(2):
        cols = slice(128 * c, 128 * c + 128)
        own = a[T * 4 * c : T * 4 * c + T, cols]
        for h in range(1, 4):
            at = T * (4 * c + h)
            own = jnp.where(lane == h, a[at : at + T, cols], own)
        halves.append(own)
    return jnp.concatenate(halves, axis=1)


def attention(w, big, q_s, k_s, v_s, p_s, o_s):
    rows = slice(w * T, w * T + T)
    half = T // 2
    if big is not None:
        query = lax.broadcasted_iota(jnp.int32, (1, 8 * T), 1) % T
        pen0 = jnp.where(query >= half, big, 0.0)
        pen1 = jnp.where(query < half, big, 0.0)
    for g in range(2):
        st = nt(k_s[g, rows, :], heads_apart(q_s[g, rows, :]))
        if big is None:
            e = jnp.exp2(st - jnp.max(st, axis=0, keepdims=True))
        else:
            top = jnp.maximum(
                jnp.max(st[:half], axis=0, keepdims=True) - pen0, jnp.max(st[half:], axis=0, keepdims=True) - pen1
            )
            e = jnp.concatenate([jnp.exp2(st[:half] - (top + pen0)), jnp.exp2(st[half:] - (top + pen1))], axis=0)
        pb = (e * (1.0 / jnp.sum(e, axis=0, keepdims=True))).astype(BF)
        p_s[w, g] = pb
        o_s[rows, 256 * g : 256 * g + 256] = heads_together(tn(pb, v_s[g, rows, :])).astype(BF)


def attention_back(w, q_s, k_s, v_s, p_s, do_s, dp_s):
    rows = slice(w * T, w * T + T)
    for g in range(2):
        kg = k_s[g, rows, :]
        qm = heads_apart(q_s[g, rows, :])
        dom = heads_apart(do_s[g, rows, :])
        dpt = nt(v_s[g, rows, :], dom)
        pb = p_s[w, g]
        p = pb.astype(F32)
        ds = (p * (dpt - jnp.sum(p * dpt, axis=0, keepdims=True))).astype(BF)
        dp_s[rows, 1024 + 256 * g : 1280 + 256 * g] = nn(pb, dom).astype(BF)
        dp_s[rows, 512 + 256 * g : 768 + 256 * g] = (nn(ds, qm) * LN2).astype(BF)
        dp_s[rows, 256 * g : 256 * g + 256] = (heads_together(tn(ds, kg)) * SCALE).astype(BF)


MESH = pl.DeviceIdType.MESH
E_AT, S_AT, C_AT, MSG = 0, 256, 368, 416
PARTS = ((E_AT, 256), (S_AT, 112), (C_AT, 48))
FREE = 3 * T


def window_of(i, j):
    if i < 3:
        return i + 3 * j
    return 6 + j


def neighbours(by):
    lon, lat = lax.axis_index("lon"), lax.axis_index("lat")
    nlon, nlat = lax.axis_size("lon"), lax.axis_size("lat")
    lon2, lat2 = lax.rem(lon + by + nlon, nlon), lax.rem(lat + by + nlat, nlat)
    return [(lon2, lat), (lon, lat2), (lon2, lat2)]


def halo_copies(which, send, recv, send_sem, recv_sem, to):
    return [
        pltpu.make_async_remote_copy(
            src_ref=send.at[which, pl.ds(at, rows)],
            dst_ref=recv.at[which, pl.ds(at, rows)],
            send_sem=send_sem.at[which, n],
            recv_sem=recv_sem.at[which, n],
            device_id=peer,
            device_id_type=MESH,
        )
        for n, ((at, rows), peer) in enumerate(zip(PARTS, to))
    ]


def kernel(
    f_any, c_any, w_any, wo_any, of_ref, df_ref, qg_ref, og_ref,
    f_ref, c_ref, w_ref, wo_ref, load_sem,
    wide, rows_s, pack, send_in, recv_in, send_out, recv_out, in_send, in_recv, out_send, out_recv,
    xw, gw, xn_s, q_s, k_s, v_s, do_s, o_s, dp_s, p_s, wt_s, wot_s,
    wg, r0, cut, t0, r1, t1, r2, t3, rs_send, rs_recv,
):
    lon, lat = lax.axis_index("lon"), lax.axis_index("lat")
    core, x, zh = lax.rem(lon, 2), lax.rem(lon // 2, 4), lon // 8
    y, zl = lax.rem(lat, 4), lat // 4
    z = zh * 2 + zl

    def at(zh_, x_, core_, zl_, y_):
        return ((zh_ * 4 + x_) * 2 + core_, zl_ * 4 + y_)

    def step(v, d):
        return lax.rem(v + d, 4)

    partner = at(zh, x, 1 - core, zl, y)
    position = {"x": x, "y": y, "z": z}
    along = {
        "x": [at(zh, step(x, d), core, zl, y) for d in (1, 2, 3)],
        "y": [at(zh, x, core, zl, step(y, d)) for d in (1, 2, 3)],
        "z": [at(step(z, d) // 2, x, core, lax.rem(step(z, d), 2), y) for d in (1, 2, 3)],
    }
    ahead, behind = neighbours(1), neighbours(-1)
    peers = ahead + behind + [partner] + along["x"] + along["y"] + along["z"]
    for m in (1, 2, 3):
        for n in (1, 2, 3):
            zn = step(z, n)
            peers.append(at(zh, step(x, m), core, zl, step(y, n)))
            peers.append(at(zn // 2, step(x, m), core, lax.rem(zn, 2), y))
            peers.append(at(zn // 2, x, core, lax.rem(zn, 2), step(y, m)))
    barrier = pltpu.get_barrier_semaphore()
    for peer in peers:
        pl.semaphore_signal(barrier, inc=1, device_id=peer, device_id_type=MESH)
    loads = [
        pltpu.make_async_copy(src, dst, load_sem.at[n])
        for n, (src, dst) in enumerate(((f_any, f_ref), (c_any, c_ref), (w_any, w_ref), (wo_any, wo_ref)))
    ]
    for load in loads:
        load.start()

    halo_in = []

    def pack_in(which, src):
        loads[which].wait()
        for l in range(2):
            for a in range(24):
                i, ar = (a - 3) // 6, (a - 3) % 6
                if a < 3:
                    row = src[l, a].astype(F32)
                    n = l * 3 + a
                    pack[S_AT + n * 12 : S_AT + n * 12 + 12] = row[6:18]
                    pack[S_AT + 72 + n * 6 : S_AT + 72 + n * 6 + 6] = row[18:24]
                    pack[C_AT + n * 6 : C_AT + n * 6 + 6] = row[0:6]
                else:
                    row = src[l, a, 0:16].astype(F32)
                    n = l * 6 + ar if i < 3 else l * 3 + ar
                    pack[E_AT + 72 * i + n * 6 : E_AT + 72 * i + n * 6 + 6] = row[0:6]
        send_in[which] = pack[...].astype(BF)

    def send(which):
        halo_in.append(halo_copies(which, send_in, recv_in, in_send, in_recv, behind))
        for copy in halo_in[-1]:
            copy.start()

    def own(which, src):
        for l in range(2):
            for a in range(3, 24):
                i, ar = (a - 3) // 6, (a - 3) % 6
                row = src[l, a].astype(F32)
                n = l * 6 + ar if i < 3 else l * 3 + ar
                wide[which, window_of(i, 0), n * 12 : n * 12 + 12] = row[6:18]
                wide[which, window_of(i, 1), n * 6 : n * 6 + 6] = row[18:24]

    pack_in(0, f_ref)
    own(0, f_ref)
    loads[2].wait()
    loads[3].wait()
    wt_s[...] = w_ref[...].T
    wot_s[...] = wo_ref[...].T
    pl.semaphore_wait(barrier, len(peers))
    send(0)
    pack_in(1, c_ref)
    own(1, c_ref)

    def project(first, count):
        rows = slice(first * T, (first + count) * T)
        for w in range(first, first + count):
            at_ = slice(w * T, w * T + T)
            xv = wide[0, w]
            xw[at_] = xv.astype(BF)
            xc, rstd = norm_stats(xv)
            xn_s[at_] = (xc * rstd).astype(BF)
        for part, (dst, scale) in enumerate(((q_s, SCALE * LOG2E), (k_s, None), (v_s, None))):
            for n in range(2):
                res = nn(xn_s[rows], w_ref[:, 512 * part + 256 * n : 512 * part + 256 * n + 256])
                if scale is not None:
                    res = res * scale
                dst[n, rows] = res.astype(BF)

    last = jnp.where(lat == lax.axis_size("lat") - 1, 1e9, 0.0)

    def attend(first, count):
        for w in range(first, first + count):
            attention(w, last if w >= NW - 2 else None, q_s, k_s, v_s, p_s, o_s)

    def project_grad(first, count):
        rows = slice(first * T, (first + count) * T)
        for w in range(first, first + count):
            gw[w * T : w * T + T] = wide[1, w].astype(BF)
        for n in range(2):
            do_s[n, rows] = nn(gw[rows], wot_s[:, 256 * n : 256 * n + 256]).astype(BF)

    def attend_back(first, count):
        for w in range(first, first + count):
            attention_back(w, q_s, k_s, v_s, p_s, do_s, dp_s)

    def finish_out(first, count):
        for w in range(first, first + count):
            at_ = slice(w * T, w * T + T)
            wide[0, w] = xw[at_].astype(F32) + nn(o_s[at_], wo_ref[...])

    def finish_grad(first, count):
        for w in range(first, first + count):
            at_ = slice(w * T, w * T + T)
            gn = nn(dp_s[at_], wt_s[...])
            xc, rstd = norm_stats(xw[at_].astype(F32))
            xh = xc * rstd
            m1 = jnp.sum(gn, axis=-1, keepdims=True) * (1.0 / D)
            m2 = jnp.sum(gn * xh, axis=-1, keepdims=True) * (1.0 / D)
            wide[1, w] = gw[at_].astype(F32) + rstd * (gn - m1 - xh * m2)

    def halo_arrived(which):
        for copy in halo_in[which]:
            copy.wait()
        pack[...] = recv_in[which].astype(F32)
        for i in range(3):
            wide[which, 3 + i, 72:144] = pack[E_AT + 72 * i : E_AT + 72 * i + 72]
        wide[which, 7, 36:72] = pack[E_AT + 216 : E_AT + 252]
        wide[which, 6, 72:144] = pack[S_AT : S_AT + 72]
        wide[which, 7, 72:108] = pack[S_AT + 72 : S_AT + 108]
        wide[which, 7, 108:144] = pack[C_AT : C_AT + 36]

    halo_out = []

    def send_back(which):
        for i in range(3):
            pack[E_AT + 72 * i : E_AT + 72 * i + 72] = wide[which, 3 + i, 72:144]
        pack[E_AT + 216 : E_AT + 252] = wide[which, 7, 36:72]
        pack[S_AT : S_AT + 72] = wide[which, 6, 72:144]
        pack[S_AT + 72 : S_AT + 108] = wide[which, 7, 72:108]
        pack[C_AT : C_AT + 36] = wide[which, 7, 108:144]
        send_out[which] = pack[...].astype(BF)
        halo_out.append(halo_copies(which, send_out, recv_out, out_send, out_recv, ahead))
        for copy in halo_out[-1]:
            copy.start()

    axes = ("y", "z", "x", "x")
    going = [None] * 4

    def rdma(b, n, src, dst, peer):
        copy = pltpu.make_async_remote_copy(
            src_ref=src, dst_ref=dst, send_sem=rs_send.at[b, n], recv_sem=rs_recv.at[b, n],
            device_id=peer, device_id_type=MESH,
        )
        copy.start()
        return copy

    def term(b):
        res = tn(xn_s[...], dp_s[:, 512 * b : 512 * b + 512]) if b < 3 else tn(o_s[...], gw[...])
        wg[b] = res.astype(BF).reshape(2, 4, 2, 2, 16, 512)
        going[b] = [rdma(b, 0, wg.at[b, :, :, 1 - core], r0.at[b], partner)]

    def pick(dims, axis, i):
        return tuple(i if dim == axis else slice(None) for dim in dims)

    def device(spot):
        return at(spot["z"] // 2, spot["x"], core, lax.rem(spot["z"], 2), spot["y"])

    def stage(b, n):
        for copy in going[b]:
            copy.wait()
        axis = axes[b]
        p, q = "zxy".replace(axis, "")
        if n == 0:
            for i in range(2):
                for k in range(4):
                    cut[i, k] = wg[b, i, k, core].astype(F32) + r0[b, i, k].astype(F32)
            for i in range(2):
                for j in range(2):
                    for k in range(4):
                        for m in range(4):
                            t3[2 * i + j, :, k, 4 * m : 4 * m + 4] = cut[i, :, j, 4 * k : 4 * k + 4, 128 * m : 128 * m + 128]
            t0[b] = t3[...].astype(BF)
            going[b] = [
                rdma(b, d, t0.at[(b, *pick("zxy", axis, step(position[axis], d)))], r1.at[b, d - 1], along[axis][d - 1])
                for d in (1, 2, 3)
            ]
        elif n == 1:
            acc = t0[(b, *pick("zxy", axis, position[axis]))].astype(F32)
            for d in range(3):
                acc = acc + r1[b, d].astype(F32)
            t1[b] = acc.astype(BF)
            going[b] = []
            for m in range(15, 0, -1):
                spot = dict(position)
                spot[p], spot[q] = step(position[p], m // 4), step(position[q], m % 4)
                going[b].append(rdma(b, 3 + m, t1.at[b, spot[p], spot[q]], r2.at[b, m - 1], device(spot)))
        else:
            acc = t1[b, position[p], position[q]].astype(F32)
            for m in range(15):
                acc = acc + r2[b, m].astype(F32)
            out, first = (qg_ref, 512 * b) if b < 3 else (og_ref, 0)
            for m in range(4):
                out[:, first + 128 * m : first + 128 * m + 128] = acc[4 * m : 4 * m + 4]

    project(0, 3)
    send(1)
    project_grad(0, 3)
    attend(0, 3)
    attend_back(0, 3)

    halo_arrived(0)
    project(3, 5)
    attend(3, 5)
    halo_arrived(1)
    project_grad(3, 5)
    term(3)
    finish_out(3, 5)
    send_back(0)
    stage(3, 0)
    attend_back(3, 5)
    finish_grad(3, 5)
    send_back(1)

    term(0)
    term(1)
    stage(0, 0)
    term(2)
    stage(1, 0)
    stage(2, 0)
    stage(3, 1)
    finish_grad(0, 3)
    finish_out(0, 3)

    def assemble(which, dst):
        for copy in halo_out[which]:
            copy.wait()
        pack[...] = recv_out[which].astype(F32)
        for l in range(2):
            for a in range(24):
                i, ar = (a - 3) // 6, (a - 3) % 6
                at_ = l * 24 + a
                if a < 3:
                    n = l * 3 + a
                    rows_s[at_, 6:18] = pack[S_AT + n * 12 : S_AT + n * 12 + 12]
                    rows_s[at_, 18:24] = pack[S_AT + 72 + n * 6 : S_AT + 72 + n * 6 + 6]
                    rows_s[at_, 0:6] = pack[C_AT + n * 6 : C_AT + n * 6 + 6]
                else:
                    n = l * 6 + ar if i < 3 else l * 3 + ar
                    rows_s[at_, 0:6] = pack[E_AT + 72 * i + n * 6 : E_AT + 72 * i + n * 6 + 6]
                    rows_s[at_, 6:18] = wide[which, window_of(i, 0), n * 12 : n * 12 + 12]
                    rows_s[at_, 18:24] = wide[which, window_of(i, 1), n * 6 : n * 6 + 6]
                dst[l, a] = rows_s[at_].astype(BF)

    assemble(0, of_ref)
    for b in range(3):
        stage(b, 1)
    stage(3, 2)
    assemble(1, df_ref)
    for b in range(3):
        stage(b, 2)


def shards(fields, cotangent, qkv_weight, out_weight):
    vm = pl.BlockSpec(memory_space=pltpu.VMEM)
    results = list(
        pl.pallas_call(
            kernel,
            out_shape=[
                pltpu.VMEM((2, 24, 24, D), BF),
                pltpu.VMEM((2, 24, 24, D), BF),
                pltpu.VMEM((4, 3 * D), F32),
                pltpu.VMEM((4, D), F32),
            ],
            in_specs=[pl.BlockSpec(memory_space=pl.ANY)] * 4,
            out_specs=[vm] * 4,
            scratch_shapes=[
                pltpu.VMEM((2, 24, 24, D), BF),
                pltpu.VMEM((2, 24, 24, D), BF),
                pltpu.VMEM((D, 3 * D), BF),
                pltpu.VMEM((D, D), BF),
                pltpu.SemaphoreType.DMA((4,)),
                pltpu.VMEM((2, NW, T, D), F32),
                pltpu.VMEM((48, 24, D), F32),
                pltpu.VMEM((MSG, D), F32),
            ]
            + [pltpu.VMEM((2, MSG, D), BF)] * 4
            + [pltpu.SemaphoreType.DMA((2, 3))] * 4
            + [pltpu.VMEM((TOK, D), BF)] * 3
            + [pltpu.VMEM((2, TOK, 256), BF)] * 4
            + [
                pltpu.VMEM((TOK, D), BF),
                pltpu.VMEM((TOK, 3 * D), BF),
                pltpu.VMEM((NW, 2, T, 8 * T), BF),
                pltpu.VMEM((3 * D, D), BF),
                pltpu.VMEM((D, D), BF),
                pltpu.VMEM((4, 2, 4, 2, 2, 16, 512), BF),
                pltpu.VMEM((4, 2, 4, 2, 16, 512), BF),
                pltpu.VMEM((2, 4, 2, 16, 512), F32),
                pltpu.VMEM((4, 4, 4, 4, 16, 128), BF),
                pltpu.VMEM((4, 3, 4, 4, 16, 128), BF),
                pltpu.VMEM((4, 4, 4, 16, 128), BF),
                pltpu.VMEM((4, 15, 16, 128), BF),
                pltpu.VMEM((4, 4, 4, 16, 128), F32),
                pltpu.SemaphoreType.DMA((4, 19)),
                pltpu.SemaphoreType.DMA((4, 19)),
            ],
            compiler_params=pltpu.CompilerParams(
                collective_id=0, has_side_effects=True, vmem_limit_bytes=58 * 1024 * 1024
            ),
            cost_estimate=pl.CostEstimate(flops=10 * 10**9, bytes_accessed=8 * 10**6, transcendentals=3 * 10**6),
        )(fields, cotangent, qkv_weight, out_weight)
    )

    def hand_over(*refs):
        copies = [pltpu.make_async_copy(refs[n], refs[4 + n], refs[8].at[n]) for n in range(4)]
        for copy in copies:
            copy.start()
        for copy in copies:
            copy.wait()

    return tuple(
        pl.pallas_call(
            hand_over,
            out_shape=[jax.ShapeDtypeStruct(r.shape, r.dtype) for r in results],
            in_specs=[vm] * 4,
            out_specs=[pl.BlockSpec(memory_space=pl.ANY)] * 4,
            scratch_shapes=[pltpu.SemaphoreType.DMA((4,))],
        )(*[pltpu.with_memory_space_constraint(r, pltpu.VMEM) for r in results])
    )


def solution(mesh):
    placed = (P(None, "lat", "lon", None), P(None, "lat", "lon", None), P(), P())
    return jax.shard_map(
        shards,
        mesh=mesh,
        in_specs=placed,
        out_specs=(
            P(None, "lat", "lon", None),
            P(None, "lat", "lon", None),
            P(("lon", "lat"), None),
            P(("lon", "lat"), None),
        ),
        check_vma=False,
    )
```
